32 devices in a mesh: dp: 4 (over x, core), expert: 8 (over z, y).
Axes of the slice: x: 2, y: 2, z: 4, core: 2. Of those that a mesh axis runs over, the one named last changes fastest.
Arguments:
- tokens: bfloat16 [4096, 3072], P(('dp', 'expert')), may hold values from -6 to 6
- target: bfloat16 [4096, 3072], P(('dp', 'expert')), may hold values from -3 to 3
- routes: int32 [4096, 1], P(('dp', 'expert')), may hold values from 0 to 7; in each aligned block of 128 rows (0 to 127, 128 to 255, ...) at most 24 rows name the same one
- thresholds: int32 [8, 2048], P('expert', 'dp'), may hold values from 0 to 3
- enc_weight: bfloat16 [8, 3072, 2048], P('expert', None, 'dp'), may hold values from -0.109375 to 0.109375
- dec_weight: bfloat16 [8, 3072, 2048], P('expert', None, 'dp'), may hold values from -0.125 to 0.125
Outputs:
- recon: bfloat16 [4096, 3072], P(('dp', 'expert'))
- grad_enc: bfloat16 [8, 3072, 2048], P('expert', None, 'dp')
- grad_dec: bfloat16 [8, 3072, 2048], P('expert', None, 'dp')
The draws below stay inside these ranges and needn't reach their ends.
Inputs may be any that keep to these rules, and one draw needn't show every extreme that they name: `routes`: within the rows of one device no expert is named by more than 24 rows, a bound that some block reaches.
All inputs are finite; a program needn't handle non-finite values.
Results may differ from the reference program's by a relative error of at most 0.012.
Values may be sent and summed in bfloat16 or wider, within the bound.
No kernel may reach another device: no remote copies, remote signals or barrier semaphores. Data moves between devices by JAX's collectives and lax.ppermute only.
A program may use at most 128 MiB of HBM per device.

```python
import math
import jax
import jax.numpy as jnp
import numpy as np
from jax import lax

D = 3072
F = 2048
TOK_DEV = 128
EXPERTS = 8
CAP = 24
TOKENS = 4096
N_DP = 4
N_EXPERT = 8


def place_ends(result, rng, smallest, top_value):
    longest = result.shape.index(max(result.shape))
    spots = []
    for shift in (0, 1):
        where = [jax.random.randint(jax.random.fold_in(rng, axis), (), 0, length) for axis, length in enumerate(result.shape)]
        where[longest] = (where[longest] + shift) % result.shape[longest]
        spots.append(tuple(where))
    return result.at[spots[0]].set(smallest).at[spots[1]].set(top_value)


def steps_of(own_key, shape, pieces, least, top_value):
    level = 1.0
    for position, parts in pieces:
        draws = jax.random.uniform(jax.random.fold_in(jax.random.fold_in(own_key, 6), position), (parts,), jnp.float32, least / len(pieces), top_value / len(pieces))
        level = level * jnp.repeat(jnp.exp(draws), shape[position] // parts).reshape((-1,) + (1,) * (len(shape) - 1 - position))
    return level


def shared_out(own_key, own, number, rows, number_of, top, bound, lean):
    sequence = jax.random.permutation(own_key, number_of)
    crowded, ordinary = load_shares(number_of, rows * top, bound, lean, True), load_shares(number_of, rows * top, bound, lean, False)
    places = jnp.arange(number_of)

    def named(sizes, turn):
        used = int((sizes > 0).sum())
        fixed = max(1, used // 4)
        moved = fixed + (places - fixed + turn * (used - fixed)) % max(1, number_of - fixed)
        return jnp.zeros((number_of,), jnp.int32).at[sequence[jnp.where(places < fixed, places, moved)]].set(jnp.asarray(sizes, jnp.int32))

    sizes = jnp.where(number % 4 == 0, named(crowded, number // 4), named(ordinary, number - number // 4 - 1))
    mixed = jax.random.permutation(jax.random.fold_in(own, 3), number_of)
    source_of, sink = mixed[0:number_of // 2 * 2:2], mixed[1:number_of // 2 * 2:2]
    margin = jnp.minimum(sizes[source_of] - 1, bound - sizes[sink]) // 2
    margin = jnp.where((source_of == sequence[0]) | (sink == sequence[0]) | (sizes[sink] == 0), 0, jnp.maximum(margin, 0))
    moved = jax.random.randint(jax.random.fold_in(own, 4), (number_of // 2,), 0, 1 << 20) % (margin + 1)
    sizes = sizes.at[source_of].add(-moved).at[sink].add(moved)
    items = jnp.searchsorted(jnp.cumsum(sizes), jnp.arange(rows * top), side="right").astype(jnp.int32)
    listing = items.reshape(top, rows).T
    listing = listing[jax.random.permutation(jax.random.fold_in(own, 1), rows)]
    turn = jax.random.randint(jax.random.fold_in(own, 2), (rows, 1), 0, top)
    return jnp.take_along_axis(listing, (jnp.arange(top)[None, :] + turn) % top, axis=1)


def load_shares(amount, total, most, skew, full):
    weights = [(1 << 20) // math.isqrt(grade ** skew) + 1 for grade in range(1, amount + 1)]
    largest = most if full else min(most, max(-(-total // amount), total * weights[0] // sum(weights)))
    least = 1 if total - largest >= amount - 1 else 0
    holding, spare = [largest] + [least] * (amount - 1), total - largest - least * (amount - 1)
    while spare > 0:
        movable = [i for i in range(1, amount) if holding[i] < largest] or [i for i in range(1, amount) if holding[i] < most]
        pool, budget = sum([weights[i] for i in movable]), spare
        for i in movable:
            addition = min(most - holding[i], max(1, budget * weights[i] // pool), spare)
            holding[i] = holding[i] + addition
            spare = spare - addition
    return np.array(holding)


def scatter_about(key, extent, width, most, cuts=(), held_as=jnp.bfloat16):
    drawn = width * jax.random.normal(key, extent, jnp.float32)
    if cuts:
        drawn = drawn * steps_of(key, extent, cuts, -0.22, 0.18)
    return jnp.clip(drawn, -most, most).astype(held_as)


def setup_inputs(seed: int = 0) -> dict:
    keys = jax.random.split(jax.random.key(seed), 7)
    tokens = scatter_about(keys[0], (TOKENS, D), 1.0, 6.0, ((0, 32),))
    target = scatter_about(keys[1], (TOKENS, D), 0.5, 3.0, ((0, 32),))
    routes_keys = jax.random.split(jax.random.fold_in(keys[2], 1), TOKENS // TOK_DEV)
    routes_turns = jax.random.permutation(jax.random.fold_in(keys[2], 3), TOKENS // TOK_DEV)
    routes = jax.vmap(lambda own, number: shared_out(jax.random.fold_in(keys[2], 2), own, number, TOK_DEV, EXPERTS, 1, CAP, 1))(routes_keys, routes_turns).reshape((TOKENS, 1))
    thresholds = place_ends(jax.random.randint(keys[3], (EXPERTS, F), 0, 4), jax.random.fold_in(keys[3], 1), 0, 3).astype(jnp.int32)
    enc_weight = scatter_about(keys[4], (EXPERTS, D, F), D ** -0.5, 0.109375, ((0, 8), (2, 4)))
    dec_weight = scatter_about(keys[5], (EXPERTS, D, F), F ** -0.5, 0.125, ((0, 8), (2, 4)))
    return {"tokens": tokens, "target": target, "routes": routes, "thresholds": thresholds, "enc_weight": enc_weight, "dec_weight": dec_weight}


error_scale = 0.03125


def clamp_parts(latent_pre):
    squash = jax.nn.sigmoid(4.0 * latent_pre)
    return latent_pre * squash, squash + 4.0 * latent_pre * squash * (1.0 - squash)


def reference(tokens, target, routes, thresholds, enc_weight, dec_weight):
    route_col = routes[:, 0]
    limit = N_DP * N_EXPERT * CAP

    def one_expert(expert_idx):
        row_index = jnp.nonzero(route_col == expert_idx, size=limit, fill_value=TOKENS)[0].astype(jnp.int32)
        present = (row_index < TOKENS)[:, None]
        rows_in = jnp.take(tokens, row_index, axis=0, mode="fill", fill_value=0)
        rows_target = jnp.take(target, row_index, axis=0, mode="fill", fill_value=0)
        shifts = 0.25 * thresholds[expert_idx].astype(jnp.float32)
        latent_pre = jnp.dot(rows_in, enc_weight[expert_idx], preferred_element_type=jnp.float32) - shifts
        value, derivative = clamp_parts(latent_pre)
        activity = value.astype(jnp.bfloat16)
        recon_rows = lax.dot_general(activity, dec_weight[expert_idx], (((1,), (1,)), ((), ())), preferred_element_type=jnp.float32).astype(jnp.bfloat16)
        error_rows = (recon_rows.astype(jnp.float32) - rows_target.astype(jnp.float32)) * error_scale
        error_rows = jnp.where(present, error_rows, jnp.float32(0.0)).astype(jnp.bfloat16)
        grad_act = jnp.dot(error_rows, dec_weight[expert_idx], preferred_element_type=jnp.float32)
        grad_pre = (grad_act * derivative).astype(jnp.bfloat16)
        grad_dec = lax.dot_general(error_rows, activity, (((0,), (0,)), ((), ())), preferred_element_type=jnp.float32).astype(jnp.bfloat16)
        grad_enc = lax.dot_general(rows_in, grad_pre, (((0,), (0,)), ((), ())), preferred_element_type=jnp.float32).astype(jnp.bfloat16)
        return grad_enc, grad_dec, recon_rows, row_index

    grad_enc, grad_dec, recon_rows, row_index = lax.map(one_expert, jnp.arange(EXPERTS, dtype=jnp.int32))
    recon = jnp.zeros((TOKENS, D), jnp.bfloat16).at[row_index.reshape(-1)].set(recon_rows.reshape(-1, D), mode="drop")
    return recon, grad_enc, grad_dec
```

```python
import functools

import jax
import jax.numpy as jnp
from jax import lax
from jax.experimental import pallas as pl
from jax.experimental.pallas import tpu as pltpu
from jax.sharding import PartitionSpec as P

error_scale = 0.03125
absent_mark = 1024.0
GROUPS = 2
f32 = jnp.float32
bf16 = jnp.bfloat16
VMEM_LIMIT = 60 * 1024 * 1024


def dot(a, b, on_a, on_b):
    return lax.dot_general(a, b, (((on_a,), (on_b,)), ((), ())), preferred_element_type=f32)


def call(kernel, name, out_shape, grid, in_specs, out_specs, scratch, flops, moved):
    return pl.pallas_call(
        kernel,
        name=name,
        out_shape=out_shape,
        grid=grid,
        in_specs=in_specs,
        out_specs=out_specs,
        scratch_shapes=scratch,
        cost_estimate=pl.CostEstimate(flops=flops, bytes_accessed=moved, transcendentals=0),
        compiler_params=pltpu.CompilerParams(
            vmem_limit_bytes=VMEM_LIMIT, dimension_semantics=("arbitrary",) * len(grid)
        ),
    )


def swap(v, distance):
    n = lax.axis_size("dp")
    return lax.ppermute(v, "dp", [(i, i ^ distance) for i in range(n)])


def pass_on(v, distance):
    n = lax.axis_size("expert")
    return lax.ppermute(v, "expert", [(i, i ^ distance) for i in range(n)])


def after(v, *first):
    return lax.optimization_barrier((v,) + first)[0]


def slot_columns(route_col, capacity):
    tokens = route_col.shape[0]
    lanes = lax.broadcasted_iota(jnp.int32, (tokens, 128), 1)
    one_hot = (route_col == lanes).astype(bf16)
    earlier = (
        lax.broadcasted_iota(jnp.int32, (tokens, tokens), 1)
        < lax.broadcasted_iota(jnp.int32, (tokens, tokens), 0)
    ).astype(bf16)
    before = dot(earlier, one_hot, 1, 0)
    rank = jnp.sum(before * one_hot.astype(f32), axis=1, keepdims=True).astype(jnp.int32)
    return route_col * capacity + rank


def place_kernel(experts, capacity, routes_ref, tokens_ref, target_ref, placing_ref, *outs):
    slot = slot_columns(routes_ref[...], capacity)
    tokens = slot.shape[0]
    slots = experts * capacity
    placing = (slot == lax.broadcasted_iota(jnp.int32, (tokens, slots), 1)).astype(f32)
    placing_ref[...] = placing.astype(bf16)
    by_slot = placing.T
    filled = jnp.sum(by_slot, axis=1, keepdims=True)
    by_slot = by_slot.astype(bf16)
    mark = (1.0 - filled) * absent_mark
    rows = dot(by_slot, tokens_ref[...], 1, 0).astype(bf16)
    wanted = (dot(by_slot, target_ref[...], 1, 0) + mark).astype(bf16)
    half = len(outs) // 2
    size = slots // half
    for k in range(half):
        outs[k][...] = rows[k * size : (k + 1) * size]
        outs[half + k][...] = wanted[k * size : (k + 1) * size]


def place(routes, tokens, target, experts, capacity):
    per_dev, features = tokens.shape
    slots = experts * capacity
    pairs = experts // 2
    size = 2 * capacity
    cut = size % 16 == 0
    count, rows = (pairs, size) if cut else (1, slots)
    steps = 2
    cols = lambda rows: pl.BlockSpec((rows, features // steps), lambda i: (0, i))
    whole = lambda *shape: pl.BlockSpec(shape, lambda i: (0, 0))
    outs = call(
        functools.partial(place_kernel, experts, capacity),
        "place",
        [jax.ShapeDtypeStruct((per_dev, slots), bf16)]
        + [jax.ShapeDtypeStruct((rows, features), bf16)] * (2 * count),
        (steps,),
        [whole(per_dev, 1), cols(per_dev), cols(per_dev)],
        [whole(per_dev, slots)] + [cols(rows)] * (2 * count),
        [],
        4 * slots * per_dev * features,
        2 * 2 * (per_dev + slots) * features,
    )(routes, tokens, target)
    boxes, wanted = outs[1 : 1 + count], outs[1 + count :]
    if not cut:
        boxes, wanted = [[v[0][size * k : size * (k + 1)] for k in range(pairs)] for v in (boxes, wanted)]
    return outs[0], boxes, wanted


def forward_kernel(steps, count, *refs):
    blocks = refs[:count]
    thr, enc, dec, act_ref, slope_ref, near_ref, far_ref, send_ref, pre = refs[count:]
    i = pl.program_id(0)
    size = act_ref.shape[0] // 4

    @pl.when(i < steps)
    def _():
        x = jnp.concatenate([b[...] for b in blocks], axis=0)
        part = dot(x, enc[...], 1, 0)

        @pl.when(i == 0)
        def _():
            pre[...] = part

        @pl.when(i > 0)
        def _():
            pre[...] += part

    @pl.when(i == steps - 1)
    def _():
        latent = pre[...] - 0.25 * thr[...].astype(f32)
        squash = jax.nn.sigmoid(4.0 * latent)
        act_ref[...] = (latent * squash).astype(bf16)
        slope_ref[...] = squash + 4.0 * latent * squash * (1.0 - squash)

    @pl.when(i >= steps)
    def _():
        part = dot(act_ref[...], dec[...], 1, 1)
        near_ref[...] = part[:size]
        send_ref[:size] = part[size : 2 * size].astype(bf16)
        far_ref[...] = part[2 * size : 3 * size]
        send_ref[size:] = part[3 * size :].astype(bf16)


def forward(blocks, thresholds, enc, dec):
    count = len(blocks)
    features = blocks[0].shape[1]
    size = sum(b.shape[0] for b in blocks) // 4
    latents = enc.shape[1]
    steps = 2
    wide = features // steps
    early = lambda i: jnp.minimum(i, steps - 1)
    late = lambda i: jnp.maximum(i - steps, 0)
    fixed = lambda *shape: pl.BlockSpec(shape, lambda i: (0, 0))
    col_out = lambda rows: pl.BlockSpec((rows, wide), lambda i: (0, late(i)))
    return call(
        functools.partial(forward_kernel, steps, count),
        "forward",
        [
            jax.ShapeDtypeStruct((4 * size, latents), bf16),
            jax.ShapeDtypeStruct((4 * size, latents), f32),
            jax.ShapeDtypeStruct((size, features), f32),
            jax.ShapeDtypeStruct((size, features), f32),
            jax.ShapeDtypeStruct((2 * size, features), bf16),
        ],
        (2 * steps,),
        [pl.BlockSpec((b.shape[0], wide), lambda i: (0, early(i))) for b in blocks]
        + [
            fixed(1, latents),
            pl.BlockSpec((wide, latents), lambda i: (early(i), 0)),
            pl.BlockSpec((wide, latents), lambda i: (late(i), 0)),
        ],
        [fixed(4 * size, latents), fixed(4 * size, latents), col_out(size), col_out(size), col_out(2 * size)],
        [pltpu.VMEM((4 * size, latents), f32)],
        2 * 2 * 4 * size * features * latents,
        4 * features * latents + 24 * size * features,
    )(*blocks, thresholds, enc, dec)


def make_error(near, got, across, wanted):
    recon = (near + got.astype(f32) + across.astype(f32)).astype(bf16)
    goal = wanted.astype(f32)
    error = (recon.astype(f32) - goal) * error_scale
    return recon, jnp.where(goal < 0.5 * absent_mark, error, 0.0).astype(bf16)


def back_kernel(steps, e0, e1, e2, e3, dec, slope, out_ref, total):
    i = pl.program_id(0)
    e = jnp.concatenate([e0[...], e1[...], e2[...], e3[...]], axis=0)
    part = dot(e, dec[...], 1, 0)

    @pl.when(i == 0)
    def _():
        total[...] = part

    @pl.when(i > 0)
    def _():
        total[...] += part

    @pl.when(i == steps - 1)
    def _():
        out_ref[...] = (total[...] * slope[...]).astype(bf16)


def back(errors, dec, slope):
    size, features = errors[0].shape
    latents = dec.shape[1]
    steps = 2
    wide = features // steps
    fixed = pl.BlockSpec((4 * size, latents), lambda i: (0, 0))
    return call(
        functools.partial(back_kernel, steps),
        "back",
        jax.ShapeDtypeStruct((4 * size, latents), bf16),
        (steps,),
        [pl.BlockSpec((size, wide), lambda i: (0, i))] * 4
        + [pl.BlockSpec((wide, latents), lambda i: (i, 0)), fixed],
        fixed,
        [pltpu.VMEM((4 * size, latents), f32)],
        2 * 4 * size * features * latents,
        2 * features * latents + 8 * size * features,
    )(*errors, dec, slope)


def weight_grad_kernel(count, *refs):
    blocks = refs[:count]
    sides = refs[count : count + GROUPS]
    out_ref = refs[-1]
    left = jnp.concatenate([b[...] for b in blocks], axis=0)
    right = jnp.concatenate([s[...] for s in sides], axis=0)
    out_ref[0] = dot(left, right, 0, 0).astype(bf16)


def weight_grad(name, blocks, sides):
    features = blocks[0].shape[1]
    size = sum(b.shape[0] for b in blocks)
    latents = sides[0].shape[1]
    wide = features // 3
    return call(
        functools.partial(weight_grad_kernel, len(blocks)),
        name,
        jax.ShapeDtypeStruct((1, features, latents), bf16),
        (features // wide,),
        [pl.BlockSpec((b.shape[0], wide), lambda i: (0, i)) for b in blocks]
        + [pl.BlockSpec(s.shape, lambda i: (0, 0)) for s in sides],
        pl.BlockSpec((1, wide, latents), lambda i: (0, i, 0)),
        [],
        2 * size * features * latents,
        2 * features * latents + 2 * size * features,
    )(*blocks, *sides)


def collect_kernel(capacity, count, placing, *refs):
    out = refs[-1]
    came = jnp.concatenate([r[...] for r in refs[:count]], axis=0)
    passed = jnp.concatenate([r[...] for r in refs[count:-1]], axis=0)
    tokens, slots = placing.shape
    lane = lax.broadcasted_iota(jnp.int32, (tokens, slots), 1)
    direct = jnp.where((lane // capacity) % 2 == 0, placing[...], jnp.zeros((), bf16))
    picks = lax.broadcasted_iota(jnp.int32, (slots, slots // 2), 0)
    place = lax.broadcasted_iota(jnp.int32, (slots, slots // 2), 1)
    source = (place // capacity) * 2 * capacity + capacity + place % capacity
    via = dot(placing[...], (picks == source).astype(bf16), 1, 0).astype(bf16)
    out[...] = (dot(direct, came, 1, 0) + dot(via, passed, 1, 0)).astype(bf16)


def collect(placing, came, passed, capacity):
    tokens, slots = placing.shape
    features = came[0].shape[1]
    steps = 2
    wide = features // steps
    cols = lambda rows: pl.BlockSpec((rows, wide), lambda i: (0, i))
    return call(
        functools.partial(collect_kernel, capacity, len(came)),
        "collect",
        jax.ShapeDtypeStruct((tokens, features), bf16),
        (steps,),
        [pl.BlockSpec((tokens, slots), lambda i: (0, 0))] + [cols(v.shape[0]) for v in came + passed],
        cols(tokens),
        [],
        3 * slots * tokens * features,
        2 * (2 * slots + tokens) * features,
    )(placing, *came, *passed)


def local(tokens, target, routes, thresholds, enc_weight, dec_weight):
    experts = lax.axis_size("expert")
    half = lax.axis_size("dp") // 2
    per_dev, features = tokens.shape
    capacity = 3 * per_dev // (2 * experts)
    enc = enc_weight[0]
    dec = dec_weight[0]
    pairs = experts // 2
    own = lax.axis_index("expert")
    placing, box, wanted_box = place(routes ^ own, tokens, target, experts, capacity)

    def outer(v, k):
        return v if k == 0 else pass_on(v, 2 * k)

    def join(arrays):
        return arrays[0] if len(arrays) == 1 else jnp.concatenate(arrays, axis=0)

    def settle(landed, *first):
        direct = [v[:capacity] for v in landed]
        via = pass_on(after(join([v[capacity:] for v in landed]), *first), 1)
        return join([v for j, d in enumerate(direct) for v in (d, via[j * capacity : (j + 1) * capacity])])

    def gather(mine):
        far = swap(mine, half)
        return [mine, swap(mine, 1), far, swap(far, 1)]

    quarter = pairs // 4
    spans = [(0, quarter), (quarter, 2 * quarter), (2 * quarter, pairs)]
    landed = [outer(box[k], k) for k in range(pairs)]
    blocks = []
    first = []
    for low, high in spans:
        mine = settle(landed[low:high], *first)
        blocks.append(gather(mine))
        first = [blocks[-1][2]]

    goal_start = (blocks[1][2], *landed[1:])
    aims = [outer(after(wanted_box[k], *goal_start), k) for k in range(pairs)]

    rows = [[b for r in range(4) for b in (blocks[0][r], blocks[1][r])], blocks[2]]
    first = blocks[2][0]
    acts, slopes, nears, gots, acrosses, sums = [], [], [], [], [], []
    for g in range(GROUPS):
        ready = [after(rows[g][0], first)] + rows[g][1:]
        act, slope, near, far, send = forward(ready, thresholds, enc, dec)
        got = swap(send, 1)
        size = near.shape[0]
        first = (far + got[size:].astype(f32)).astype(bf16)
        acts.append(act)
        slopes.append(slope)
        nears.append(near)
        gots.append(got[:size])
        sums.append(first)
        acrosses.append(swap(first, half))

    spans = [(0, 2 * quarter), (2 * quarter, pairs)]
    errors, homes = [], []
    first = (acts[1], blocks[2][3])
    for g, (low, high) in enumerate(spans):
        wanted = settle(aims[low:high], acts[0])
        recon, error = make_error(nears[g], gots[g], after(acrosses[g], *first), wanted)
        homes += [outer(recon[2 * capacity * j : 2 * capacity * (j + 1)], low + j) for j in range(high - low)]
        errors.append(gather(error))
        first = (error,)

    grad_pres = []
    first = errors[1][0]
    for g in range(GROUPS):
        ready = [after(errors[g][0], first)] + errors[g][1:]
        grad_pres.append(back(ready, dec, slopes[g]))
        first = grad_pres[-1]
    passed = []
    for (low, high), first in zip(spans, (errors[1][0], grad_pres[1])):
        passed.append(pass_on(after(join([v[capacity:] for v in homes[low:high]]), first), 1))
    came = [join(homes[i * quarter : (i + 1) * quarter]) for i in range(4)]
    flat = lambda groups: [b for group in groups for b in group]
    grad_dec = weight_grad("grad_dec", flat(errors), acts)
    grad_enc = weight_grad("grad_enc", flat(rows), grad_pres)
    recon = collect(after(placing, grad_enc), came, passed, capacity)
    return recon, grad_enc, grad_dec


def solution(mesh):
    in_specs = (
        P(("dp", "expert"), None),
        P(("dp", "expert"), None),
        P(("dp", "expert"), None),
        P("expert", "dp"),
        P("expert", None, "dp"),
        P("expert", None, "dp"),
    )
    out_specs = (P(("dp", "expert"), None), P("expert", None, "dp"), P("expert", None, "dp"))
    return jax.shard_map(local, mesh=mesh, in_specs=in_specs, out_specs=out_specs, check_vma=False)
```

```python
import functools

import jax
import jax.numpy as jnp
from jax import lax
from jax.experimental import pallas as pl
from jax.experimental.pallas import tpu as pltpu
from jax.sharding import PartitionSpec as P

error_scale = 0.03125
absent_mark = 1024.0
GROUPS = 2
f32 = jnp.float32
bf16 = jnp.bfloat16
VMEM_LIMIT = 60 * 1024 * 1024
WEIGH = 10


def dot(a, b, on_a, on_b):
    return lax.dot_general(a, b, (((on_a,), (on_b,)), ((), ())), preferred_element_type=f32)


def call(kernel, name, out_shape, grid, in_specs, out_specs, scratch, flops, moved):
    return pl.pallas_call(
        kernel,
        name=name,
        out_shape=out_shape,
        grid=grid,
        in_specs=in_specs,
        out_specs=out_specs,
        scratch_shapes=scratch,
        cost_estimate=pl.CostEstimate(flops=WEIGH * flops, bytes_accessed=WEIGH * moved, transcendentals=0),
        compiler_params=pltpu.CompilerParams(
            vmem_limit_bytes=VMEM_LIMIT, dimension_semantics=("arbitrary",) * len(grid)
        ),
    )


def swap(v, distance):
    n = lax.axis_size("dp")
    return lax.ppermute(v, "dp", [(i, i ^ distance) for i in range(n)])


def pass_on(v, distance):
    n = lax.axis_size("expert")
    return lax.ppermute(v, "expert", [(i, i ^ distance) for i in range(n)])


def after(v, *first):
    return lax.optimization_barrier((v,) + first)[0]


def gate(values, *first):
    return list(lax.optimization_barrier(tuple(values) + first)[: len(values)])


def slot_row(route_row, capacity, pairs):
    tokens = route_row.shape[1]
    distance = route_row ^ lax.axis_index("expert")
    one_hot = (lax.broadcasted_iota(jnp.int32, (2 * pairs, tokens), 0) == distance).astype(f32)
    earlier = (
        lax.broadcasted_iota(jnp.int32, (tokens, tokens), 0)
        < lax.broadcasted_iota(jnp.int32, (tokens, tokens), 1)
    ).astype(bf16)
    before = dot(one_hot.astype(bf16), earlier, 1, 0)
    rank = jnp.sum(before * one_hot, axis=0, keepdims=True).astype(jnp.int32)
    return ((distance & 1) * pairs + (distance >> 1)) * capacity + rank


def store_parts(rows, outs):
    start = 0
    for out in outs:
        out[...] = rows[start : start + out.shape[0]].astype(bf16)
        start += out.shape[0]


def place_kernel(capacity, pairs, routes_ref, tokens_ref, by_slot_ref, *outs):
    slots, tokens = by_slot_ref.shape
    slot = slot_row(routes_ref[...], capacity, pairs)
    by_slot = (lax.broadcasted_iota(jnp.int32, (slots, tokens), 0) == slot).astype(f32).astype(bf16)
    by_slot_ref[...] = by_slot
    store_parts(dot(by_slot, tokens_ref[...], 1, 0), outs)


def place_target_kernel(by_slot_ref, target_ref, *outs):
    by_slot = by_slot_ref[...]
    mark = (1.0 - jnp.sum(by_slot.astype(f32), axis=1, keepdims=True)) * absent_mark
    store_parts(dot(by_slot, target_ref[...], 1, 0) + mark, outs)


def place(name, kernel, first, values, slots, pairs, with_slots):
    per_dev, features = values.shape
    capacity = slots // (2 * pairs)
    sizes = [capacity] * pairs if capacity % 8 == 0 else [slots // 2]
    sizes = sizes + [slots // 2]
    steps = 2
    cols = lambda rows: pl.BlockSpec((rows, features // steps), lambda i: (0, i))
    whole = lambda *shape: pl.BlockSpec(shape, lambda i: (0, 0))
    outs = call(
        kernel,
        name,
        [jax.ShapeDtypeStruct((slots, per_dev), bf16)] * with_slots
        + [jax.ShapeDtypeStruct((size, features), bf16) for size in sizes],
        (steps,),
        [whole(*first.shape), cols(per_dev)],
        [whole(slots, per_dev)] * with_slots + [cols(size) for size in sizes],
        [],
        2 * slots * per_dev * features,
        2 * (per_dev + slots) * features,
    )(first, values)
    direct, via = outs[with_slots:-1], outs[-1]
    if len(direct) == 1:
        direct = [direct[0][capacity * k : capacity * (k + 1)] for k in range(pairs)]
    return outs[0], list(direct), via


def forward_kernel(steps, count, *refs):
    blocks = refs[:count]
    thr, enc, dec, act_ref, slope_ref, near_ref, far_ref, send_near_ref, send_far_ref, pre = refs[count:]
    i = pl.program_id(0)
    size = act_ref.shape[0] // 4

    @pl.when(i < steps)
    def _():
        x = jnp.concatenate([b[...] for b in blocks], axis=0)
        part = dot(x, enc[...], 1, 0)

        @pl.when(i == 0)
        def _():
            pre[...] = part

        @pl.when(i > 0)
        def _():
            pre[...] += part

    @pl.when(i == steps - 1)
    def _():
        latent = pre[...] - 0.25 * thr[...].astype(f32)
        squash = jax.nn.sigmoid(4.0 * latent)
        act_ref[...] = (latent * squash).astype(bf16)
        slope_ref[...] = squash + 4.0 * latent * squash * (1.0 - squash)

    @pl.when(i >= steps)
    def _():
        part = dot(act_ref[...], dec[...], 1, 1)
        near_ref[...] = part[:size]
        send_near_ref[...] = part[size : 2 * size].astype(bf16)
        far_ref[...] = part[2 * size : 3 * size]
        send_far_ref[...] = part[3 * size :].astype(bf16)


def forward(blocks, thresholds, enc, dec):
    count = len(blocks)
    features = blocks[0].shape[1]
    size = sum(b.shape[0] for b in blocks) // 4
    latents = enc.shape[1]
    steps = 2
    wide = features // steps
    early = lambda i: jnp.minimum(i, steps - 1)
    late = lambda i: jnp.maximum(i - steps, 0)
    fixed = lambda *shape: pl.BlockSpec(shape, lambda i: (0, 0))
    col_out = lambda rows: pl.BlockSpec((rows, wide), lambda i: (0, late(i)))
    return call(
        functools.partial(forward_kernel, steps, count),
        "forward",
        [
            jax.ShapeDtypeStruct((4 * size, latents), bf16),
            jax.ShapeDtypeStruct((4 * size, latents), f32),
            jax.ShapeDtypeStruct((size, features), f32),
            jax.ShapeDtypeStruct((size, features), f32),
            jax.ShapeDtypeStruct((size, features), bf16),
            jax.ShapeDtypeStruct((size, features), bf16),
        ],
        (2 * steps,),
        [pl.BlockSpec((b.shape[0], wide), lambda i: (0, early(i))) for b in blocks]
        + [
            fixed(1, latents),
            pl.BlockSpec((wide, latents), lambda i: (early(i), 0)),
            pl.BlockSpec((wide, latents), lambda i: (late(i), 0)),
        ],
        [fixed(4 * size, latents), fixed(4 * size, latents), *[col_out(size)] * 4],
        [pltpu.VMEM((4 * size, latents), f32)],
        2 * 2 * 4 * size * features * latents,
        4 * features * latents + 24 * size * features,
    )(*blocks, thresholds, enc, dec)


def make_error(near, got, across, wanted):
    recon = (near + got.astype(f32) + across.astype(f32)).astype(bf16)
    goal = wanted.astype(f32)
    error = (recon.astype(f32) - goal) * error_scale
    return recon, jnp.where(goal < 0.5 * absent_mark, error, 0.0).astype(bf16)


def back_kernel(steps, e0, e1, e2, e3, dec, slope, out_ref, total):
    i = pl.program_id(0)
    e = jnp.concatenate([e0[...], e1[...], e2[...], e3[...]], axis=0)
    part = dot(e, dec[...], 1, 0)

    @pl.when(i == 0)
    def _():
        total[...] = part

    @pl.when(i > 0)
    def _():
        total[...] += part

    @pl.when(i == steps - 1)
    def _():
        out_ref[...] = (total[...] * slope[...]).astype(bf16)


def back(errors, dec, slope):
    size, features = errors[0].shape
    latents = dec.shape[1]
    steps = 2
    wide = features // steps
    fixed = pl.BlockSpec((4 * size, latents), lambda i: (0, 0))
    return call(
        functools.partial(back_kernel, steps),
        "back",
        jax.ShapeDtypeStruct((4 * size, latents), bf16),
        (steps,),
        [pl.BlockSpec((size, wide), lambda i: (0, i))] * 4
        + [pl.BlockSpec((wide, latents), lambda i: (i, 0)), fixed],
        fixed,
        [pltpu.VMEM((4 * size, latents), f32)],
        2 * 4 * size * features * latents,
        2 * features * latents + 8 * size * features,
    )(*errors, dec, slope)


def weight_grad_kernel(count, *refs):
    blocks = refs[:count]
    sides = refs[count : count + GROUPS]
    out_ref = refs[-1]
    left = jnp.concatenate([b[...] for b in blocks], axis=0)
    right = jnp.concatenate([s[...] for s in sides], axis=0)
    out_ref[0] = dot(left, right, 0, 0).astype(bf16)


def weight_grad(name, blocks, sides):
    features = blocks[0].shape[1]
    size = sum(b.shape[0] for b in blocks)
    latents = sides[0].shape[1]
    wide = features // 3
    return call(
        functools.partial(weight_grad_kernel, len(blocks)),
        name,
        jax.ShapeDtypeStruct((1, features, latents), bf16),
        (features // wide,),
        [pl.BlockSpec((b.shape[0], wide), lambda i: (0, i)) for b in blocks]
        + [pl.BlockSpec(s.shape, lambda i: (0, 0)) for s in sides],
        pl.BlockSpec((1, wide, latents), lambda i: (0, i, 0)),
        [],
        2 * size * features * latents,
        2 * features * latents + 2 * size * features,
    )(*blocks, *sides)


def collect_kernel(by_slot, direct, via, out):
    out[...] = dot(by_slot[...], jnp.concatenate([direct[...], via[...]], axis=0), 0, 0).astype(bf16)


def collect(by_slot, direct, via):
    slots, tokens = by_slot.shape
    features = direct.shape[1]
    steps = 2
    cols = lambda rows: pl.BlockSpec((rows, features // steps), lambda i: (0, i))
    return call(
        collect_kernel,
        "collect",
        jax.ShapeDtypeStruct((tokens, features), bf16),
        (steps,),
        [pl.BlockSpec((slots, tokens), lambda i: (0, 0)), cols(slots // 2), cols(slots // 2)],
        cols(tokens),
        [],
        2 * slots * tokens * features,
        2 * (slots + tokens) * features,
    )(by_slot, direct, via)


def local(tokens, target, routes, thresholds, enc_weight, dec_weight):
    experts = lax.axis_size("expert")
    half = lax.axis_size("dp") // 2
    per_dev, features = tokens.shape
    capacity = 3 * per_dev // (2 * experts)
    enc = enc_weight[0]
    dec = dec_weight[0]
    pairs = experts // 2
    slots = experts * capacity
    by_slot, direct, via = place(
        "place",
        functools.partial(place_kernel, capacity, pairs),
        routes.reshape(1, per_dev),
        tokens,
        slots,
        pairs,
        True,
    )
    _, goal_direct, goal_via = place(
        "place_target", place_target_kernel, by_slot, target, slots, pairs, False
    )

    def spread(parts):
        return [parts[0]] + [pass_on(parts[k], 2 * k) for k in range(1, pairs)]

    def cut(v):
        return [v[capacity * k : capacity * (k + 1)] for k in range(pairs)]

    def join(arrays):
        return jnp.concatenate(arrays, axis=0)

    def encode(blocks):
        return forward(blocks, thresholds, enc, dec)

    def total(far, got):
        return (far + got.astype(f32)).astype(bf16)

    out_direct = spread(direct)
    out_via = pass_on(via, 1)
    *out_direct, out_via, goal_via = gate(out_direct + [out_via, goal_via])
    mine0 = join(out_direct)
    out_via = spread(cut(out_via))
    far0 = swap(mine0, half)
    goal_via = pass_on(goal_via, 1)
    *out_via, mine0, far0, goal_via = gate(out_via + [mine0, far0, goal_via])
    goal_direct = gate(goal_direct, far0)
    mine1 = join(out_via)
    far1 = swap(mine1, half)
    goal_direct = spread(goal_direct)
    blocks0 = [mine0, swap(mine0, 1), far0, swap(far0, 1)]
    act0, slope0, keep0, other0, send_near0, send_far0 = encode(blocks0)
    *goal_direct, mine1, far1, send_near0, send_far0, goal_via = gate(
        goal_direct + [mine1, far1, send_near0, send_far0, goal_via]
    )
    across0 = swap(total(other0, swap(send_far0, 1)), half)
    goal_via = spread(cut(goal_via))
    blocks1 = [mine1, swap(mine1, 1), far1, swap(far1, 1)]
    act1, slope1, keep1, other1, send_near1, send_far1 = encode(blocks1)
    *goal_via, across0, send_near0, send_near1, send_far1 = gate(
        goal_via + [across0, send_near0, send_near1, send_far1]
    )
    across1 = swap(total(other1, swap(send_far1, 1)), half)
    recon0, error0 = make_error(keep0, swap(send_near0, 1), across0, join(goal_direct))
    home0 = spread(cut(recon0))
    *home0, across1, error0, send_near1 = gate(home0 + [across1, error0, send_near1])
    efar0 = swap(error0, half)
    recon1, error1 = make_error(keep1, swap(send_near1, 1), across1, join(goal_via))
    home1 = spread(cut(recon1))
    *home1, error0, efar0, error1 = gate(home1 + [error0, efar0, error1])
    efar1, enear1 = swap(error1, half), swap(error1, 1)
    home1 = pass_on(join(home1), 1)
    errors0 = [error0, swap(error0, 1), efar0, swap(efar0, 1)]
    back0 = back(errors0, dec, slope0)
    home1, efar1, enear1, back0 = gate([home1, efar1, enear1, back0])
    errors1 = [error1, enear1, efar1, swap(efar1, 1)]
    back1 = back(errors1, dec, slope1)
    grad_dec = weight_grad("grad_dec", errors0 + errors1, [act0, act1])
    grad_enc = weight_grad("grad_enc", blocks0 + blocks1, [back0, back1])
    recon = collect(by_slot, join(home0), home1)
    return recon, grad_enc, grad_dec


def solution(mesh):
    in_specs = (
        P(("dp", "expert"), None),
        P(("dp", "expert"), None),
        P(("dp", "expert"), None),
        P("expert", "dp"),
        P("expert", None, "dp"),
        P("expert", None, "dp"),
    )
    out_specs = (P(("dp", "expert"), None), P("expert", None, "dp"), P("expert", None, "dp"))
    return jax.shard_map(local, mesh=mesh, in_specs=in_specs, out_specs=out_specs, check_vma=False)
```

```python
import functools

import jax
import jax.numpy as jnp
from jax import lax
from jax.experimental import pallas as pl
from jax.experimental.pallas import tpu as pltpu
from jax.sharding import PartitionSpec as P

error_scale = 0.03125
absent_mark = 1024.0
GROUPS = 2
f32 = jnp.float32
bf16 = jnp.bfloat16
VMEM_LIMIT = 36 * 1024 * 1024
WEIGH = 10


def dot(a, b, on_a, on_b):
    return lax.dot_general(a, b, (((on_a,), (on_b,)), ((), ())), preferred_element_type=f32)


def call(kernel, name, out_shape, grid, in_specs, out_specs, scratch, flops, moved):
    return pl.pallas_call(
        kernel,
        name=name,
        out_shape=out_shape,
        grid=grid,
        in_specs=in_specs,
        out_specs=out_specs,
        scratch_shapes=scratch,
        cost_estimate=pl.CostEstimate(flops=WEIGH * flops, bytes_accessed=WEIGH * moved, transcendentals=0),
        compiler_params=pltpu.CompilerParams(
            vmem_limit_bytes=VMEM_LIMIT, dimension_semantics=("arbitrary",) * len(grid) or None
        ),
    )


def swap(v, distance):
    n = lax.axis_size("dp")
    return lax.ppermute(v, "dp", [(i, i ^ distance) for i in range(n)])


def pass_on(v, distance):
    n = lax.axis_size("expert")
    return lax.ppermute(v, "expert", [(i, i ^ distance) for i in range(n)])


def after(v, *first):
    return lax.optimization_barrier((v,) + first)[0]


def gate(values, *first):
    return list(lax.optimization_barrier(tuple(values) + first)[: len(values)])


def slot_row(route_row, capacity, pairs):
    tokens = route_row.shape[1]
    distance = route_row ^ lax.axis_index("expert")
    one_hot = (lax.broadcasted_iota(jnp.int32, (2 * pairs, tokens), 0) == distance).astype(f32)
    earlier = (
        lax.broadcasted_iota(jnp.int32, (tokens, tokens), 0)
        < lax.broadcasted_iota(jnp.int32, (tokens, tokens), 1)
    ).astype(bf16)
    before = dot(one_hot.astype(bf16), earlier, 1, 0)
    rank = jnp.sum(before * one_hot, axis=0, keepdims=True).astype(jnp.int32)
    return ((distance & 1) * pairs + (distance >> 1)) * capacity + rank


def store_parts(rows, outs):
    start = 0
    for out in outs:
        out[...] = rows[start : start + out.shape[0]].astype(bf16)
        start += out.shape[0]


def place_kernel(capacity, pairs, routes_ref, tokens_ref, by_slot_ref, *outs):
    slots, tokens = by_slot_ref.shape
    slot = slot_row(routes_ref[...], capacity, pairs)
    by_slot = (lax.broadcasted_iota(jnp.int32, (slots, tokens), 0) == slot).astype(f32).astype(bf16)
    by_slot_ref[...] = by_slot
    store_parts(dot(by_slot, tokens_ref[...], 1, 0), outs)


def place_target_kernel(by_slot_ref, target_ref, *outs):
    by_slot = by_slot_ref[...]
    mark = (1.0 - jnp.sum(by_slot.astype(f32), axis=1, keepdims=True)) * absent_mark
    store_parts(dot(by_slot, target_ref[...], 1, 0) + mark, outs)


def place(name, kernel, first, values, slots, pairs, with_slots):
    per_dev, features = values.shape
    capacity = slots // (2 * pairs)
    sizes = [capacity] * pairs if capacity % 8 == 0 else [slots // 2]
    sizes = sizes + [slots // 2]
    steps = 2
    cols = lambda rows: pl.BlockSpec((rows, features // steps), lambda i: (0, i))
    whole = lambda *shape: pl.BlockSpec(shape, lambda i: (0, 0))
    outs = call(
        kernel,
        name,
        [jax.ShapeDtypeStruct((slots, per_dev), bf16)] * with_slots
        + [jax.ShapeDtypeStruct((size, features), bf16) for size in sizes],
        (steps,),
        [whole(*first.shape), cols(per_dev)],
        [whole(slots, per_dev)] * with_slots + [cols(size) for size in sizes],
        [],
        2 * slots * per_dev * features,
        2 * (per_dev + slots) * features,
    )(first, values)
    direct, via = outs[with_slots:-1], outs[-1]
    if len(direct) == 1:
        direct = [direct[0][capacity * k : capacity * (k + 1)] for k in range(pairs)]
    return outs[0], list(direct), via


def clamp_parts(latent):
    squash = jax.nn.sigmoid(4.0 * latent)
    return (latent * squash).astype(bf16), squash + 4.0 * latent * squash * (1.0 - squash)


def forward_kernel(
    steps, mine, far, shift, shift_o, enc, enc_o, dec, dec_o, rows, pre, pre_o, keep, out, act, act_o
):
    i = pl.program_id(0)
    size = mine.shape[0]

    @pl.when(i < steps)
    def _():
        x = jnp.concatenate([mine[...], far[...]], axis=0)
        rows[...] = x
        part, part_o = dot(x, enc[...], 1, 0), dot(x, enc_o[...], 1, 0)

        @pl.when(i == 0)
        def _():
            pre[...] = part - shift[...]
            pre_o[...] = part_o - shift_o[...]

        @pl.when(i > 0)
        def _():
            pre[...] += part
            pre_o[...] += part_o

    @pl.when(i == steps - 1)
    def _():
        act[...] = clamp_parts(pre[...])[0]
        act_o[...] = clamp_parts(pre_o[...])[0]

    @pl.when(i >= steps)
    def _():
        part = dot(act[...], dec[...], 1, 1) + dot(act_o[...], dec_o[...], 1, 1)
        keep[...] = part[:size]
        out[...] = part[size:].astype(bf16)


def forward(mine, far, shifts, encs, decs):
    size, features = mine.shape
    latents = encs[0].shape[1]
    steps = 2
    wide = features // steps
    early = lambda i: jnp.minimum(i, steps - 1)
    late = lambda i: jnp.maximum(i - steps, 0)
    col_in = lambda rows: pl.BlockSpec((rows, wide), lambda i: (0, early(i)))
    fixed = lambda *shape: pl.BlockSpec(shape, lambda i: (0, 0))
    col_out = pl.BlockSpec((size, wide), lambda i: (0, late(i)))
    enc_in = pl.BlockSpec((wide, latents), lambda i: (early(i), 0))
    dec_in = pl.BlockSpec((wide, latents), lambda i: (late(i), 0))
    return call(
        functools.partial(forward_kernel, steps),
        "forward",
        [
            jax.ShapeDtypeStruct((2 * size, features), bf16),
            jax.ShapeDtypeStruct((2 * size, latents), f32),
            jax.ShapeDtypeStruct((2 * size, latents), f32),
            jax.ShapeDtypeStruct((size, features), f32),
            jax.ShapeDtypeStruct((size, features), bf16),
        ],
        (2 * steps,),
        [col_in(size)] * 2 + [fixed(1, latents)] * 2 + [enc_in] * 2 + [dec_in] * 2,
        [col_in(2 * size), fixed(2 * size, latents), fixed(2 * size, latents), col_out, col_out],
        [pltpu.VMEM((2 * size, latents), bf16)] * 2,
        2 * 2 * 4 * size * features * latents,
        8 * features * latents + 14 * size * features,
    )(mine, far, *shifts, *encs, *decs)


def make_error(keep, across, wanted):
    recon = (keep + across.astype(f32)).astype(bf16)
    goal = wanted.astype(f32)
    error = (recon.astype(f32) - goal) * error_scale
    return recon, jnp.where(goal < 0.5 * absent_mark, error, 0.0).astype(bf16)


def gradients_kernel(tiles, summed, *refs):
    errors, rows = refs[:4], refs[4:6]
    act, slope, dec = refs[6:9]
    before = refs[9:11] if summed else ()
    out_enc, out_dec = refs[9 + len(before) : 11 + len(before)]
    e_all, x_all, act_all, slope_all, dec_all, was, out_buf, sems, out_sems = refs[11 + len(before) :]
    features = errors[0].shape[1]
    cut = features // 2
    wide = features // tiles
    started = []

    def fetch(source, target):
        copy = pltpu.make_async_copy(source, target, sems.at[len(started)])
        copy.start()
        started.append(copy)
        return copy

    def fetch_rows(refs, target, columns):
        size = refs[0].shape[0]
        return [
            fetch(r.at[:, columns], target.at[pl.ds(size * j, size), columns]) for j, r in enumerate(refs)
        ]

    first = []
    for columns in (pl.ds(0, cut), pl.ds(cut, cut)):
        first.append(fetch_rows(errors, e_all, columns) + [fetch(dec.at[columns, :], dec_all.at[columns, :])])
    first[1].append(fetch(slope, slope_all))
    second = [fetch(act, act_all)]
    second += [fetch(before[1].at[0], was.at[1])] if summed else []
    third = fetch_rows(rows, x_all, pl.ds(0, features))
    third += [fetch(before[0].at[0], was.at[0])] if summed else []

    total = None
    for columns, copies in zip((slice(0, cut), slice(cut, features)), first):
        for copy in copies:
            copy.wait()
        part = dot(e_all[:, columns], dec_all[columns, :], 1, 0)
        total = part if total is None else total + part
    pre = (total * slope_all[...]).astype(bf16)

    pending = {}
    for n, (left, out, copies) in enumerate(((x_all, out_enc, third), (e_all, out_dec, second))[::-1]):
        for copy in copies:
            copy.wait()
        right = act_all[...] if n == 0 else pre
        for i in range(tiles):
            slot = (n * tiles + i) % 3
            if slot in pending:
                pending.pop(slot).wait()
            here = slice(i * wide, (i + 1) * wide)
            part = dot(left[:, here], right, 0, 0)
            if summed:
                part = part + was[1 - n, here, :].astype(f32)
            out_buf[slot] = part.astype(bf16)
            pending[slot] = pltpu.make_async_copy(
                out_buf.at[slot], out.at[0, pl.ds(i * wide, wide), :], out_sems.at[slot]
            )
            pending[slot].start()
    for copy in pending.values():
        copy.wait()


def gradients(errors, rows, act, slope, dec, before):
    size, features = errors[0].shape
    latents = dec.shape[1]
    tiles = 3
    summed = len(before) > 0
    anywhere = pl.BlockSpec(memory_space=pl.ANY)
    was = (2, features, latents) if summed else (2, 16, 128)
    return call(
        functools.partial(gradients_kernel, tiles, summed),
        "gradients_sum" if summed else "gradients",
        [jax.ShapeDtypeStruct((1, features, latents), bf16)] * 2,
        (),
        [anywhere] * (9 + len(before)),
        [anywhere] * 2,
        [
            pltpu.VMEM((4 * size, features), bf16),
            pltpu.VMEM((4 * size, features), bf16),
            pltpu.VMEM((4 * size, latents), bf16),
            pltpu.VMEM((4 * size, latents), f32),
            pltpu.VMEM((features, latents), bf16),
            pltpu.VMEM(was, bf16),
            pltpu.VMEM((3, features // tiles, latents), bf16),
            pltpu.SemaphoreType.DMA((16,)),
            pltpu.SemaphoreType.DMA((3,)),
        ],
        2 * 12 * size * features * latents,
        6 * features * latents + 32 * size * features,
    )(*errors, *rows, act, slope, dec, *before)


def collect_kernel(by_slot, direct, via, out):
    out[...] = dot(by_slot[...], jnp.concatenate([direct[...], via[...]], axis=0), 0, 0).astype(bf16)


def collect(by_slot, direct, via):
    slots, tokens = by_slot.shape
    features = direct.shape[1]
    steps = 2
    cols = lambda rows: pl.BlockSpec((rows, features // steps), lambda i: (0, i))
    return call(
        collect_kernel,
        "collect",
        jax.ShapeDtypeStruct((tokens, features), bf16),
        (steps,),
        [pl.BlockSpec((slots, tokens), lambda i: (0, 0)), cols(slots // 2), cols(slots // 2)],
        cols(tokens),
        [],
        2 * slots * tokens * features,
        2 * (slots + tokens) * features,
    )(by_slot, direct, via)


def local(tokens, target, routes, thresholds, enc_weight, dec_weight):
    experts = lax.axis_size("expert")
    half = lax.axis_size("dp") // 2
    per_dev, features = tokens.shape
    capacity = 3 * per_dev // (2 * experts)
    enc = enc_weight[0]
    dec = dec_weight[0]
    pairs = experts // 2
    slots = experts * capacity
    by_slot, direct, via = place(
        "place",
        functools.partial(place_kernel, capacity, pairs),
        routes.reshape(1, per_dev),
        tokens,
        slots,
        pairs,
        True,
    )
    _, goal_direct, goal_via = place(
        "place_target", place_target_kernel, by_slot, target, slots, pairs, False
    )

    def spread(parts, step=0):
        return [pass_on(v, 2 * k + step) if 2 * k + step else v for k, v in enumerate(parts)]

    def cut(v):
        return [v[capacity * k : capacity * (k + 1)] for k in range(pairs)]

    def join(arrays):
        return jnp.concatenate(arrays, axis=0)

    shift = 0.25 * thresholds.astype(f32)
    shift_o = swap(shift, 1)

    def gradient_side(pre, got):
        return clamp_parts(jnp.concatenate([pre, got], axis=0))

    out_direct = spread(direct)
    out_via = pass_on(via, 1)
    enc_o = swap(enc, 1)
    *out_direct, out_via, goal_via, shift_o, enc_o = gate(out_direct + [out_via, goal_via, shift_o, enc_o])
    mine0 = join(out_direct)
    out_via = spread(cut(out_via))
    far0 = swap(mine0, half)
    dec_o = swap(after(dec, enc_o), 1)
    *out_via, mine0, far0, goal_via, dec_o = gate(out_via + [mine0, far0, goal_via, dec_o])
    goal_direct = gate(goal_direct, dec_o)
    shifts, encs, decs = (shift, shift_o), (enc, enc_o), (dec, dec_o)
    mine1 = join(out_via)
    far1 = swap(mine1, half)
    goal_direct = spread(goal_direct)
    goal_via = pass_on(goal_via, 1)
    rows0, pre0, pre_o0, keep0, sum0 = forward(mine0, far0, shifts, encs, decs)
    *goal_direct, mine1, far1, keep0, sum0, goal_via, pre_o0 = gate(
        goal_direct + [mine1, far1, keep0, sum0, goal_via, pre_o0]
    )
    across0 = swap(sum0, half)
    got0 = swap(pre_o0, 1)
    goal_via = spread(cut(after(goal_via, got0)))
    rows1, pre1, pre_o1, keep1, sum1 = forward(mine1, far1, shifts, encs, decs)
    *goal_via, across0, sum1, got0, pre_o1, rows0 = gate(goal_via + [across0, sum1, got0, pre_o1, rows0])
    across1 = swap(sum1, half)
    recon0, error0 = make_error(keep0, across0, join(goal_direct))
    home0 = spread(cut(recon0))
    got1 = swap(pre_o1, 1)
    act0, slope0 = gradient_side(pre0, got0)
    *home0, across1, error0, got1, slope0 = gate(home0 + [across1, error0, got1, slope0])
    efar0 = swap(error0, half)
    recon1, error1 = make_error(keep1, across1, join(goal_via))
    home_via = cut(recon1)
    home1 = [pass_on(home_via[k], 2 * k + 1) for k in range(1, pairs)]
    act1, slope1 = gradient_side(pre1, got1)
    *home1, home_via[0], error0, efar0, error1, slope1, rows0, rows1 = gate(
        home1 + [home_via[0], error0, efar0, error1, slope1, rows0, rows1]
    )
    efar1 = swap(error1, half)
    home1 = [pass_on(home_via[0], 1)] + home1
    errors0 = [error0, efar0, swap(error0, 1), swap(efar0, 1)]
    before = gradients(errors0, [rows0, swap(rows0, 1)], act0, slope0, dec, ())
    core1 = swap(after(rows1, errors0[3]), 1)
    enear1 = swap(after(error1, errors0[3]), 1)
    homes = gate([join(home0), join(home1)], before[0])
    recon = collect(by_slot, *homes)
    efar1, enear1, recon, core1, *before = gate([efar1, enear1, recon, core1, *before])
    errors1 = [error1, efar1, enear1, swap(efar1, 1)]
    grad_enc, grad_dec = gradients(errors1, [rows1, core1], act1, slope1, dec, before)
    return recon, grad_enc, grad_dec


def solution(mesh):
    in_specs = (
        P(("dp", "expert"), None),
        P(("dp", "expert"), None),
        P(("dp", "expert"), None),
        P("expert", "dp"),
        P("expert", None, "dp"),
        P("expert", None, "dp"),
    )
    out_specs = (P(("dp", "expert"), None), P("expert", None, "dp"), P("expert", None, "dp"))
    return jax.shard_map(local, mesh=mesh, in_specs=in_specs, out_specs=out_specs, check_vma=False)
```

```python
import functools

import jax
import jax.numpy as jnp
from jax import lax
from jax.experimental import pallas as pl
from jax.experimental.pallas import tpu as pltpu
from jax.sharding import PartitionSpec as P

error_scale = 0.03125
absent_mark = 1024.0
GROUPS = 2
f32 = jnp.float32
bf16 = jnp.bfloat16
VMEM_LIMIT = 36 * 1024 * 1024
WEIGH = 10


def dot(a, b, on_a, on_b):
    return lax.dot_general(a, b, (((on_a,), (on_b,)), ((), ())), preferred_element_type=f32)


def call(kernel, name, out_shape, grid, in_specs, out_specs, scratch, flops, moved):
    return pl.pallas_call(
        kernel,
        name=name,
        out_shape=out_shape,
        grid=grid,
        in_specs=in_specs,
        out_specs=out_specs,
        scratch_shapes=scratch,
        cost_estimate=pl.CostEstimate(flops=WEIGH * flops, bytes_accessed=WEIGH * moved, transcendentals=0),
        compiler_params=pltpu.CompilerParams(
            vmem_limit_bytes=VMEM_LIMIT, dimension_semantics=("arbitrary",) * len(grid) or None
        ),
    )


def swap(v, distance):
    n = lax.axis_size("dp")
    return lax.ppermute(v, "dp", [(i, i ^ distance) for i in range(n)])


def pass_on(v, distance):
    n = lax.axis_size("expert")
    return lax.ppermute(v, "expert", [(i, i ^ distance) for i in range(n)])


def after(v, *first):
    return lax.optimization_barrier((v,) + first)[0]


def gate(values, *first):
    return list(lax.optimization_barrier(tuple(values) + first)[: len(values)])


def slot_row(route_row, capacity, pairs):
    tokens = route_row.shape[1]
    distance = route_row ^ lax.axis_index("expert")
    one_hot = (lax.broadcasted_iota(jnp.int32, (2 * pairs, tokens), 0) == distance).astype(f32)
    earlier = (
        lax.broadcasted_iota(jnp.int32, (tokens, tokens), 0)
        < lax.broadcasted_iota(jnp.int32, (tokens, tokens), 1)
    ).astype(bf16)
    before = dot(one_hot.astype(bf16), earlier, 1, 0)
    rank = jnp.sum(before * one_hot, axis=0, keepdims=True).astype(jnp.int32)
    return ((distance & 1) * pairs + (pairs - (distance >> 1)) % pairs) * capacity + rank


def store_parts(rows, outs):
    start = 0
    for out in outs:
        out[...] = rows[start : start + out.shape[0]].astype(bf16)
        start += out.shape[0]


def place_kernel(capacity, pairs, routes_ref, tokens_ref, by_slot_ref, *outs):
    slots, tokens = by_slot_ref.shape
    slot = slot_row(routes_ref[...], capacity, pairs)
    by_slot = (lax.broadcasted_iota(jnp.int32, (slots, tokens), 0) == slot).astype(f32).astype(bf16)
    by_slot_ref[...] = by_slot
    store_parts(dot(by_slot, tokens_ref[...], 1, 0), outs)


def place_target_kernel(by_slot_ref, target_ref, *outs):
    by_slot = by_slot_ref[...]
    mark = (1.0 - jnp.sum(by_slot.astype(f32), axis=1, keepdims=True)) * absent_mark
    store_parts(dot(by_slot, target_ref[...], 1, 0) + mark, outs)


def place(name, kernel, first, values, sizes, with_slots):
    per_dev, features = values.shape
    slots = sum(sizes)
    wanted = sizes
    if any(size % 8 for size in sizes):
        sizes = [slots]
    steps = 2
    cols = lambda rows: pl.BlockSpec((rows, features // steps), lambda i: (0, i))
    whole = lambda *shape: pl.BlockSpec(shape, lambda i: (0, 0))
    outs = call(
        kernel,
        name,
        [jax.ShapeDtypeStruct((slots, per_dev), bf16)] * with_slots
        + [jax.ShapeDtypeStruct((size, features), bf16) for size in sizes],
        (steps,),
        [whole(*first.shape), cols(per_dev)],
        [whole(slots, per_dev)] * with_slots + [cols(size) for size in sizes],
        [],
        2 * slots * per_dev * features,
        2 * (per_dev + slots) * features,
    )(first, values)
    parts = list(outs[with_slots:])
    if len(parts) < len(wanted):
        starts = [sum(wanted[:j]) for j in range(len(wanted))]
        parts = [parts[0][start : start + size] for start, size in zip(starts, wanted)]
    return outs[0], parts


def clamp_parts(latent):
    squash = jax.nn.sigmoid(4.0 * latent)
    return (latent * squash).astype(bf16), squash + 4.0 * latent * squash * (1.0 - squash)


def forward_kernel(
    steps, mine, far, shift, shift_o, enc, enc_o, dec, dec_o, pre, pre_o, keep, out, act, act_o
):
    i = pl.program_id(0)
    size = mine.shape[0]

    @pl.when(i < steps)
    def _():
        x = jnp.concatenate([mine[...], far[...]], axis=0)
        part, part_o = dot(x, enc[...], 1, 0), dot(x, enc_o[...], 1, 0)

        @pl.when(i == 0)
        def _():
            pre[...] = part - shift[...]
            pre_o[...] = part_o - shift_o[...]

        @pl.when(i > 0)
        def _():
            pre[...] += part
            pre_o[...] += part_o

    @pl.when(i == steps - 1)
    def _():
        act[...] = clamp_parts(pre[...])[0]
        act_o[...] = clamp_parts(pre_o[...])[0]

    @pl.when(i >= steps)
    def _():
        part = dot(act[...], dec[...], 1, 1) + dot(act_o[...], dec_o[...], 1, 1)
        keep[...] = part[:size]
        out[...] = part[size:].astype(bf16)


def forward(mine, far, shifts, encs, decs):
    size, features = mine.shape
    latents = encs[0].shape[1]
    steps = 2
    wide = features // steps
    early = lambda i: jnp.minimum(i, steps - 1)
    late = lambda i: jnp.maximum(i - steps, 0)
    col_in = lambda rows: pl.BlockSpec((rows, wide), lambda i: (0, early(i)))
    fixed = lambda *shape: pl.BlockSpec(shape, lambda i: (0, 0))
    col_out = pl.BlockSpec((size, wide), lambda i: (0, late(i)))
    enc_in = pl.BlockSpec((wide, latents), lambda i: (early(i), 0))
    dec_in = pl.BlockSpec((wide, latents), lambda i: (late(i), 0))
    return call(
        functools.partial(forward_kernel, steps),
        "forward",
        [
            jax.ShapeDtypeStruct((2 * size, latents), f32),
            jax.ShapeDtypeStruct((2 * size, latents), f32),
            jax.ShapeDtypeStruct((size, features), f32),
            jax.ShapeDtypeStruct((size, features), bf16),
        ],
        (2 * steps,),
        [col_in(size)] * 2 + [fixed(1, latents)] * 2 + [enc_in] * 2 + [dec_in] * 2,
        [fixed(2 * size, latents), fixed(2 * size, latents), col_out, col_out],
        [pltpu.VMEM((2 * size, latents), bf16)] * 2,
        2 * 2 * 4 * size * features * latents,
        8 * features * latents + 14 * size * features,
    )(mine, far, *shifts, *encs, *decs)


def make_error(keep, across, wanted):
    recon = (keep + across.astype(f32)).astype(bf16)
    goal = wanted.astype(f32)
    error = (recon.astype(f32) - goal) * error_scale
    return recon, jnp.where(goal < 0.5 * absent_mark, error, 0.0).astype(bf16)


def gradients_kernel(tiles, count, *refs):
    errors, rows = refs[:count], refs[count : 2 * count]
    half = count // 2
    acts, slopes = refs[2 * count : 2 * count + half], refs[2 * count + half : 3 * count]
    dec, *rest = refs[3 * count :]
    summed = len(rest) > 4
    before, rest = (rest[:2], rest[2:]) if summed else ((), rest)
    act = jnp.concatenate([a[...] for a in acts], axis=0)
    slope = jnp.concatenate([s[...] for s in slopes], axis=0)
    out_enc, out_dec, out_buf, out_sems = rest
    features = errors[0].shape[1]
    wide = features // tiles
    cuts = [slice(i * wide, (i + 1) * wide) for i in range(tiles)]
    stack = lambda refs, cut: jnp.concatenate([r[:, cut] for r in refs], axis=0)

    pending = {}

    def put(n, i, left, right, out, was):
        slot = (n * tiles + i) % 3
        if slot in pending:
            pending.pop(slot).wait()
        part = dot(left, right, 0, 0)
        if summed:
            part = part + was[0, cuts[i], :].astype(f32)
        out_buf[slot] = part.astype(bf16)
        pending[slot] = pltpu.make_async_copy(
            out_buf.at[slot], out.at[0, pl.ds(i * wide, wide), :], out_sems.at[slot]
        )
        pending[slot].start()

    total = None
    for i, cut in enumerate(cuts):
        left = stack(errors, cut)
        part = dot(left, dec[cut, :], 1, 0)
        total = part if total is None else total + part
        put(0, i, left, act, out_dec, before[1] if summed else None)
    pre = (total * slope).astype(bf16)
    for i, cut in enumerate(cuts):
        put(1, i, stack(rows, cut), pre, out_enc, before[0] if summed else None)
    for copy in pending.values():
        copy.wait()


def gradients(errors, rows, acts, slopes, dec, before):
    size, features = errors[0].shape
    latents = dec.shape[1]
    tiles = 3
    count = len(errors)
    summed = len(before) > 0
    return call(
        functools.partial(gradients_kernel, tiles, count),
        "gradients_sum" if summed else "gradients",
        [jax.ShapeDtypeStruct((1, features, latents), bf16)] * 2,
        (),
        [pl.BlockSpec(memory_space=pltpu.VMEM)] * (3 * count + 1 + len(before)),
        [pl.BlockSpec(memory_space=pl.ANY)] * 2,
        [
            pltpu.VMEM((3, features // tiles, latents), bf16),
            pltpu.SemaphoreType.DMA((3,)),
        ],
        2 * 3 * count * size * features * latents,
        6 * features * latents + 4 * count * size * features,
    )(*errors, *rows, *acts, *slopes, dec, *before)


def collect_kernel(by_slot, direct, via, out):
    out[...] = dot(by_slot[...], jnp.concatenate([direct[...], via[...]], axis=0), 0, 0).astype(bf16)


def collect(by_slot, direct, via):
    slots, tokens = by_slot.shape
    features = direct.shape[1]
    steps = 2
    cols = lambda rows: pl.BlockSpec((rows, features // steps), lambda i: (0, i))
    return call(
        collect_kernel,
        "collect",
        jax.ShapeDtypeStruct((tokens, features), bf16),
        (steps,),
        [pl.BlockSpec((slots, tokens), lambda i: (0, 0)), cols(slots // 2), cols(slots // 2)],
        cols(tokens),
        [],
        2 * slots * tokens * features,
        2 * (slots + tokens) * features,
    )(by_slot, direct, via)


def local(tokens, target, routes, thresholds, enc_weight, dec_weight):
    experts = lax.axis_size("expert")
    half = lax.axis_size("dp") // 2
    per_dev, features = tokens.shape
    capacity = 3 * per_dev // (2 * experts)
    enc = enc_weight[0]
    dec = dec_weight[0]
    pairs = experts // 2
    sizes = [capacity] * pairs + [pairs * capacity]
    by_slot, parts = place(
        "place",
        functools.partial(place_kernel, capacity, pairs),
        routes.reshape(1, per_dev),
        tokens,
        sizes,
        True,
    )
    direct, via = parts[:pairs], parts[pairs]
    _, parts = place(
        "place_target",
        place_target_kernel,
        by_slot,
        target,
        sizes,
        False,
    )
    goal_direct, goal_via = parts[:pairs], parts[pairs]

    def outer(v, k, step=0):
        distance = 2 * ((pairs - k) % pairs) + step
        return pass_on(v, distance) if distance else v

    def spread(parts):
        return [outer(v, k) for k, v in enumerate(parts)]

    def cut(v):
        return [v[capacity * k : capacity * (k + 1)] for k in range(pairs)]

    def join(arrays):
        return jnp.concatenate(arrays, axis=0)

    shift = 0.25 * thresholds.astype(f32)
    shift_o = swap(shift, 1)

    def gradient_sides(pre, got):
        size = pre.shape[0] // 2
        sides = [clamp_parts(jnp.concatenate([pre[c], got[c]], axis=0)) for c in (slice(size), slice(size, None))]
        return [v for side in sides for v in side]

    out_direct = spread(direct)
    out_via = pass_on(via, 1)
    enc_o = swap(enc, 1)
    *out_direct, out_via, goal_via, shift_o, enc_o = gate(out_direct + [out_via, goal_via, shift_o, enc_o])
    mine0 = join(out_direct)
    out_via = spread(cut(out_via))
    far0 = swap(mine0, half)
    dec_o = swap(after(dec, enc_o), 1)
    *out_via, mine0, far0, goal_via, dec_o = gate(out_via + [mine0, far0, goal_via, dec_o])
    shifts, encs, decs = (shift, shift_o), (enc, enc_o), (dec, dec_o)
    mine1 = join(out_via)
    far1, cmine0 = swap(mine1, half), swap(mine0, 1)
    goal_direct = spread(gate(goal_direct, dec_o, cmine0))
    goal_via = pass_on(goal_via, 1)
    pre0, pre_o0, keep0, sum0 = forward(after(mine0, cmine0), far0, shifts, encs, decs)
    *goal_direct, mine1, far1, far0, keep0, sum0, goal_via, pre_o0 = gate(
        goal_direct + [mine1, far1, far0, keep0, sum0, goal_via, pre_o0]
    )
    across0 = swap(sum0, half)
    got0, cfar0 = swap(pre_o0, 1), swap(far0, 1)
    goal_via = spread(cut(after(goal_via, got0, cfar0)))
    pre1, pre_o1, keep1, sum1 = forward(after(mine1, got0, cfar0), far1, shifts, encs, decs)
    *goal_via, across0, sum1, got0, pre_o1 = gate(goal_via + [across0, sum1, got0, pre_o1])
    across1 = swap(sum1, half)
    recon0, error0 = make_error(keep0, across0, join(goal_direct))
    home0 = spread(cut(recon0))
    got1 = swap(pre_o1, 1)
    sides0 = gradient_sides(pre0, got0)
    *home0, across1, error0, got1, sides0[0] = gate(home0 + [across1, error0, got1, sides0[0]])
    efar0, enear0 = swap(error0, half), swap(error0, 1)
    recon1, error1 = make_error(keep1, across1, join(goal_via))
    home_via = cut(after(recon1, enear0))
    home1 = [outer(home_via[k], k, 1) for k in range(1, pairs)]
    sides1 = gradient_sides(pre1, got1)
    *home1, home_via, error0, efar0, error1, sides1[0], mine1, far1 = gate(
        home1 + [home_via[0], error0, efar0, error1, sides1[0], mine1, far1]
    )
    efar1 = swap(error1, half)
    ecross0, enear1, cmine1 = swap(efar0, 1), swap(error1, 1), swap(mine1, 1)
    home_via, far1 = gate([home_via, far1], ecross0, enear1, cmine1)
    home1 = [pass_on(home_via, 1)] + home1
    cfar1 = swap(far1, 1)
    before = gradients(
        [error0, enear0, efar0, ecross0, error1, enear1],
        [mine0, cmine0, far0, cfar0, mine1, cmine1],
        [sides0[0], sides0[2], sides1[0]],
        [sides0[1], sides0[3], sides1[1]],
        dec,
        (),
    )
    efar1, cfar1, *before = gate([efar1, cfar1, *before])
    ecross1 = swap(efar1, 1)
    homes = gate([join(home0), join(home1)], efar1)
    recon = collect(by_slot, *homes)
    grad_enc, grad_dec = gradients(
        [efar1, ecross1], [far1, cfar1], [sides1[2]], [sides1[3]], dec, before
    )
    return recon, grad_enc, grad_dec


def solution(mesh):
    in_specs = (
        P(("dp", "expert"), None),
        P(("dp", "expert"), None),
        P(("dp", "expert"), None),
        P("expert", "dp"),
        P("expert", None, "dp"),
        P("expert", None, "dp"),
    )
    out_specs = (P(("dp", "expert"), None), P("expert", None, "dp"), P("expert", None, "dp"))
    return jax.shard_map(local, mesh=mesh, in_specs=in_specs, out_specs=out_specs, check_vma=False)
```

```python
import functools

import jax
import jax.numpy as jnp
from jax import lax
from jax.experimental import pallas as pl
from jax.experimental.pallas import tpu as pltpu
from jax.sharding import PartitionSpec as P

error_scale = 0.03125
absent_mark = 1024.0
GROUPS = 2
f32 = jnp.float32
bf16 = jnp.bfloat16
VMEM_LIMIT = 36 * 1024 * 1024
WEIGH = 10


def dot(a, b, on_a, on_b):
    return lax.dot_general(a, b, (((on_a,), (on_b,)), ((), ())), preferred_element_type=f32)


def call(kernel, name, out_shape, grid, in_specs, out_specs, scratch, flops, moved):
    return pl.pallas_call(
        kernel,
        name=name,
        out_shape=out_shape,
        grid=grid,
        in_specs=in_specs,
        out_specs=out_specs,
        scratch_shapes=scratch,
        cost_estimate=pl.CostEstimate(flops=WEIGH * flops, bytes_accessed=WEIGH * moved, transcendentals=0),
        compiler_params=pltpu.CompilerParams(
            vmem_limit_bytes=VMEM_LIMIT, dimension_semantics=("arbitrary",) * len(grid) or None
        ),
    )


def swap(v, distance):
    n = lax.axis_size("dp")
    return lax.ppermute(v, "dp", [(i, i ^ distance) for i in range(n)])


def pass_on(v, distance):
    n = lax.axis_size("expert")
    return lax.ppermute(v, "expert", [(i, i ^ distance) for i in range(n)])


def after(v, *first):
    return lax.optimization_barrier((v,) + first)[0]


def gate(values, *first):
    return list(lax.optimization_barrier(tuple(values) + first)[: len(values)])


def slot_row(route_row, capacity, pairs):
    tokens = route_row.shape[1]
    distance = route_row ^ lax.axis_index("expert")
    one_hot = (lax.broadcasted_iota(jnp.int32, (2 * pairs, tokens), 0) == distance).astype(f32)
    earlier = (
        lax.broadcasted_iota(jnp.int32, (tokens, tokens), 0)
        < lax.broadcasted_iota(jnp.int32, (tokens, tokens), 1)
    ).astype(bf16)
    before = dot(one_hot.astype(bf16), earlier, 1, 0)
    rank = jnp.sum(before * one_hot, axis=0, keepdims=True).astype(jnp.int32)
    return ((distance & 1) * pairs + (pairs - (distance >> 1)) % pairs) * capacity + rank


def store_parts(rows, outs):
    start = 0
    for out in outs:
        out[...] = rows[start : start + out.shape[0]].astype(bf16)
        start += out.shape[0]


def place_kernel(capacity, pairs, routes_ref, tokens_ref, by_slot_ref, *outs):
    slots, tokens = by_slot_ref.shape
    slot = slot_row(routes_ref[...], capacity, pairs)
    by_slot = (lax.broadcasted_iota(jnp.int32, (slots, tokens), 0) == slot).astype(f32).astype(bf16)
    by_slot_ref[...] = by_slot
    store_parts(dot(by_slot, tokens_ref[...], 1, 0), outs)


def place_target_kernel(by_slot_ref, target_ref, *outs):
    by_slot = by_slot_ref[...]
    mark = (1.0 - jnp.sum(by_slot.astype(f32), axis=1, keepdims=True)) * absent_mark
    store_parts(dot(by_slot, target_ref[...], 1, 0) + mark, outs)


def place(name, kernel, first, values, sizes, with_slots):
    per_dev, features = values.shape
    slots = sum(sizes)
    wanted = sizes
    if any(size % 8 for size in sizes):
        sizes = [slots]
    steps = 2
    cols = lambda rows: pl.BlockSpec((rows, features // steps), lambda i: (0, i))
    whole = lambda *shape: pl.BlockSpec(shape, lambda i: (0, 0))
    outs = call(
        kernel,
        name,
        [jax.ShapeDtypeStruct((slots, per_dev), bf16)] * with_slots
        + [jax.ShapeDtypeStruct((size, features), bf16) for size in sizes],
        (steps,),
        [whole(*first.shape), cols(per_dev)],
        [whole(slots, per_dev)] * with_slots + [cols(size) for size in sizes],
        [],
        2 * slots * per_dev * features,
        2 * (per_dev + slots) * features,
    )(first, values)
    parts = list(outs[with_slots:])
    if len(parts) < len(wanted):
        starts = [sum(wanted[:j]) for j in range(len(wanted))]
        parts = [parts[0][start : start + size] for start, size in zip(starts, wanted)]
    return outs[0], parts


def clamp_parts(latent):
    squash = jax.nn.sigmoid(4.0 * latent)
    return (latent * squash).astype(bf16), squash + 4.0 * latent * squash * (1.0 - squash)


def forward_kernel(
    steps, mine, far, shift, shift_o, enc, enc_o, dec, dec_o, pre, pre_o, keep, out, act, act_o
):
    i = pl.program_id(0)
    size = mine.shape[0]

    @pl.when(i < steps)
    def _():
        x = jnp.concatenate([mine[...], far[...]], axis=0)
        part, part_o = dot(x, enc[...], 1, 0), dot(x, enc_o[...], 1, 0)

        @pl.when(i == 0)
        def _():
            pre[...] = part - shift[...]
            pre_o[...] = part_o - shift_o[...]

        @pl.when(i > 0)
        def _():
            pre[...] += part
            pre_o[...] += part_o

    @pl.when(i == steps - 1)
    def _():
        act[...] = clamp_parts(pre[...])[0]
        act_o[...] = clamp_parts(pre_o[...])[0]

    @pl.when(i >= steps)
    def _():
        part = dot(act[...], dec[...], 1, 1) + dot(act_o[...], dec_o[...], 1, 1)
        keep[...] = part[:size]
        out[...] = part[size:].astype(bf16)


def forward(mine, far, shifts, encs, decs):
    size, features = mine.shape
    latents = encs[0].shape[1]
    steps = 2
    wide = features // steps
    early = lambda i: jnp.minimum(i, steps - 1)
    late = lambda i: jnp.maximum(i - steps, 0)
    col_in = lambda rows: pl.BlockSpec((rows, wide), lambda i: (0, early(i)))
    fixed = lambda *shape: pl.BlockSpec(shape, lambda i: (0, 0))
    col_out = pl.BlockSpec((size, wide), lambda i: (0, late(i)))
    enc_in = pl.BlockSpec((wide, latents), lambda i: (early(i), 0))
    dec_in = pl.BlockSpec((wide, latents), lambda i: (late(i), 0))
    return call(
        functools.partial(forward_kernel, steps),
        "forward",
        [
            jax.ShapeDtypeStruct((2 * size, latents), f32),
            jax.ShapeDtypeStruct((2 * size, latents), f32),
            jax.ShapeDtypeStruct((size, features), f32),
            jax.ShapeDtypeStruct((size, features), bf16),
        ],
        (2 * steps,),
        [col_in(size)] * 2 + [fixed(1, latents)] * 2 + [enc_in] * 2 + [dec_in] * 2,
        [fixed(2 * size, latents), fixed(2 * size, latents), col_out, col_out],
        [pltpu.VMEM((2 * size, latents), bf16)] * 2,
        2 * 2 * 4 * size * features * latents,
        8 * features * latents + 14 * size * features,
    )(mine, far, *shifts, *encs, *decs)


def make_error(keep, across, wanted):
    recon = (keep + across.astype(f32)).astype(bf16)
    goal = wanted.astype(f32)
    error = (recon.astype(f32) - goal) * error_scale
    return recon, jnp.where(goal < 0.5 * absent_mark, error, 0.0).astype(bf16)


def gradients_kernel(tiles, count, *refs):
    errors, rows = refs[:count], refs[count : 2 * count]
    half = count // 2
    acts, slopes = refs[2 * count : 2 * count + half], refs[2 * count + half : 3 * count]
    dec, *rest = refs[3 * count :]
    summed = len(rest) > 4
    before, rest = (rest[:2], rest[2:]) if summed else ((), rest)
    act = jnp.concatenate([a[...] for a in acts], axis=0)
    slope = jnp.concatenate([s[...] for s in slopes], axis=0)
    out_enc, out_dec, out_buf, out_sems = rest
    features = errors[0].shape[1]
    wide = features // tiles
    cuts = [slice(i * wide, (i + 1) * wide) for i in range(tiles)]
    stack = lambda refs, cut: jnp.concatenate([r[:, cut] for r in refs], axis=0)

    pending = {}

    def put(n, i, left, right, out, was):
        slot = (n * tiles + i) % 3
        if slot in pending:
            pending.pop(slot).wait()
        part = dot(left, right, 0, 0)
        if summed:
            part = part + was[0, cuts[i], :].astype(f32)
        out_buf[slot] = part.astype(bf16)
        pending[slot] = pltpu.make_async_copy(
            out_buf.at[slot], out.at[0, pl.ds(i * wide, wide), :], out_sems.at[slot]
        )
        pending[slot].start()

    total = None
    for i, cut in enumerate(cuts):
        left = stack(errors, cut)
        part = dot(left, dec[cut, :], 1, 0)
        total = part if total is None else total + part
        put(0, i, left, act, out_dec, before[1] if summed else None)
    pre = (total * slope).astype(bf16)
    for i, cut in enumerate(cuts):
        put(1, i, stack(rows, cut), pre, out_enc, before[0] if summed else None)
    for copy in pending.values():
        copy.wait()


def gradients(errors, rows, acts, slopes, dec, before):
    size, features = errors[0].shape
    latents = dec.shape[1]
    tiles = 3
    count = len(errors)
    summed = len(before) > 0
    return call(
        functools.partial(gradients_kernel, tiles, count),
        "gradients_sum" if summed else "gradients",
        [jax.ShapeDtypeStruct((1, features, latents), bf16)] * 2,
        (),
        [pl.BlockSpec(memory_space=pltpu.VMEM)] * (3 * count + 1 + len(before)),
        [pl.BlockSpec(memory_space=pl.ANY)] * 2,
        [
            pltpu.VMEM((3, features // tiles, latents), bf16),
            pltpu.SemaphoreType.DMA((3,)),
        ],
        2 * 3 * count * size * features * latents,
        6 * features * latents + 4 * count * size * features,
    )(*errors, *rows, *acts, *slopes, dec, *before)


def collect_kernel(by_slot, direct, via, out):
    out[...] = dot(by_slot[...], jnp.concatenate([direct[...], via[...]], axis=0), 0, 0).astype(bf16)


def collect(by_slot, direct, via):
    slots, tokens = by_slot.shape
    features = direct.shape[1]
    steps = 2
    cols = lambda rows: pl.BlockSpec((rows, features // steps), lambda i: (0, i))
    return call(
        collect_kernel,
        "collect",
        jax.ShapeDtypeStruct((tokens, features), bf16),
        (steps,),
        [pl.BlockSpec((slots, tokens), lambda i: (0, 0)), cols(slots // 2), cols(slots // 2)],
        cols(tokens),
        [],
        2 * slots * tokens * features,
        2 * (slots + tokens) * features,
    )(by_slot, direct, via)


def local(tokens, target, routes, thresholds, enc_weight, dec_weight):
    experts = lax.axis_size("expert")
    half = lax.axis_size("dp") // 2
    per_dev, features = tokens.shape
    capacity = 3 * per_dev // (2 * experts)
    enc = enc_weight[0]
    dec = dec_weight[0]
    pairs = experts // 2
    sizes = [capacity] * pairs + [pairs * capacity]
    by_slot, parts = place(
        "place",
        functools.partial(place_kernel, capacity, pairs),
        routes.reshape(1, per_dev),
        tokens,
        sizes,
        True,
    )
    direct, via = parts[:pairs], parts[pairs]
    _, parts = place(
        "place_target",
        place_target_kernel,
        by_slot,
        target,
        sizes,
        False,
    )
    goal_direct, goal_via = parts[:pairs], parts[pairs]

    def outer(v, k, step=0):
        distance = 2 * ((pairs - k) % pairs) + step
        return pass_on(v, distance) if distance else v

    def spread(parts):
        return [outer(v, k) for k, v in enumerate(parts)]

    def cut(v):
        return [v[capacity * k : capacity * (k + 1)] for k in range(pairs)]

    def join(arrays):
        return jnp.concatenate(arrays, axis=0)

    shift = 0.25 * thresholds.astype(f32)
    shift_o = swap(shift, 1)

    def gradient_sides(pre, got):
        size = pre.shape[0] // 2
        sides = [clamp_parts(jnp.concatenate([pre[c], got[c]], axis=0)) for c in (slice(size), slice(size, None))]
        return [v for side in sides for v in side]

    out_direct = spread(direct)
    out_via = pass_on(via, 1)
    enc_o = swap(enc, 1)
    *out_direct, out_via, goal_via, shift_o, enc_o = gate(out_direct + [out_via, goal_via, shift_o, enc_o])
    mine0 = join(out_direct)
    out_via = spread(cut(out_via))
    far0 = swap(mine0, half)
    dec_o = swap(after(dec, enc_o), 1)
    *out_via, mine0, far0, goal_via, dec_o = gate(out_via + [mine0, far0, goal_via, dec_o])
    shifts, encs, decs = (shift, shift_o), (enc, enc_o), (dec, dec_o)
    mine1 = join(out_via)
    far1 = swap(mine1, half)
    goal_direct = spread(gate(goal_direct, dec_o))
    goal_via = pass_on(goal_via, 1)
    pre0, pre_o0, keep0, sum0 = forward(mine0, far0, shifts, encs, decs)
    *goal_direct, mine1, far1, far0, keep0, sum0, goal_via, pre_o0 = gate(
        goal_direct + [mine1, far1, far0, keep0, sum0, goal_via, pre_o0]
    )
    across0 = swap(sum0, half)
    got0 = swap(pre_o0, 1)
    goal_via = spread(cut(after(goal_via, got0)))
    pre1, pre_o1, keep1, sum1 = forward(after(mine1, got0), far1, shifts, encs, decs)
    *goal_via, across0, sum1, got0, pre_o1, mine1 = gate(goal_via + [across0, sum1, got0, pre_o1, mine1])
    across1 = swap(sum1, half)
    recon0, error0 = make_error(keep0, across0, join(goal_direct))
    home0 = spread(cut(recon0))
    got1 = swap(pre_o1, 1)
    sides0 = gradient_sides(pre0, got0)
    *home0, across1, error0, got1, sides0[0] = gate(home0 + [across1, error0, got1, sides0[0]])
    efar0, enear0 = swap(error0, half), swap(error0, 1)
    cfar0, cmine0 = swap(far0, 1), swap(mine0, 1)
    recon1, error1 = make_error(keep1, across1, join(goal_via))
    home_via = cut(recon1)
    home1 = [outer(home_via[k], k, 1) for k in range(1, pairs)]
    sides1 = gradient_sides(pre1, got1)
    *home1, home_via, error0, efar0, cfar0, cmine0, error1, sides1[0], mine1, far1 = gate(
        home1 + [home_via[0], error0, efar0, cfar0, cmine0, error1, sides1[0], mine1, far1]
    )
    efar1 = swap(error1, half)
    ecross0, enear1, cmine1 = swap(efar0, 1), swap(error1, 1), swap(mine1, 1)
    home_via, far1 = gate([home_via, far1], ecross0, enear1)
    home1 = [pass_on(home_via, 1)] + home1
    cfar1 = swap(far1, 1)
    before = gradients(
        [error0, enear0, efar0, ecross0, error1, enear1],
        [mine0, cmine0, far0, cfar0, mine1, cmine1],
        [sides0[0], sides0[2], sides1[0]],
        [sides0[1], sides0[3], sides1[1]],
        dec,
        (),
    )
    efar1, cfar1, *before = gate([efar1, cfar1, *before])
    ecross1 = swap(efar1, 1)
    homes = gate([join(home0), join(home1)], efar1)
    recon = collect(by_slot, *homes)
    grad_enc, grad_dec = gradients(
        [efar1, ecross1], [far1, cfar1], [sides1[2]], [sides1[3]], dec, before
    )
    return recon, grad_enc, grad_dec


def solution(mesh):
    in_specs = (
        P(("dp", "expert"), None),
        P(("dp", "expert"), None),
        P(("dp", "expert"), None),
        P("expert", "dp"),
        P("expert", None, "dp"),
        P("expert", None, "dp"),
    )
    out_specs = (P(("dp", "expert"), None), P("expert", None, "dp"), P("expert", None, "dp"))
    return jax.shard_map(local, mesh=mesh, in_specs=in_specs, out_specs=out_specs, check_vma=False)
```

```python
import functools

import jax
import jax.numpy as jnp
from jax import lax
from jax.experimental import pallas as pl
from jax.experimental.pallas import tpu as pltpu
from jax.sharding import PartitionSpec as P

error_scale = 0.03125
absent_mark = 1024.0
GROUPS = 2
f32 = jnp.float32
bf16 = jnp.bfloat16
VMEM_LIMIT = 36 * 1024 * 1024
WEIGH = 10


def dot(a, b, on_a, on_b):
    return lax.dot_general(a, b, (((on_a,), (on_b,)), ((), ())), preferred_element_type=f32)


def call(kernel, name, out_shape, grid, in_specs, out_specs, scratch, flops, moved):
    return pl.pallas_call(
        kernel,
        name=name,
        out_shape=out_shape,
        grid=grid,
        in_specs=in_specs,
        out_specs=out_specs,
        scratch_shapes=scratch,
        cost_estimate=pl.CostEstimate(flops=WEIGH * flops, bytes_accessed=WEIGH * moved, transcendentals=0),
        compiler_params=pltpu.CompilerParams(
            vmem_limit_bytes=VMEM_LIMIT, dimension_semantics=("arbitrary",) * len(grid) or None
        ),
    )


def swap(v, distance):
    n = lax.axis_size("dp")
    return lax.ppermute(v, "dp", [(i, i ^ distance) for i in range(n)])


def pass_on(v, distance):
    n = lax.axis_size("expert")
    return lax.ppermute(v, "expert", [(i, i ^ distance) for i in range(n)])


def after(v, *first):
    return lax.optimization_barrier((v,) + first)[0]


def gate(values, *first):
    return list(lax.optimization_barrier(tuple(values) + first)[: len(values)])


def slot_row(route_row, capacity, pairs):
    tokens = route_row.shape[1]
    distance = route_row ^ lax.axis_index("expert")
    one_hot = (lax.broadcasted_iota(jnp.int32, (2 * pairs, tokens), 0) == distance).astype(f32)
    earlier = (
        lax.broadcasted_iota(jnp.int32, (tokens, tokens), 0)
        < lax.broadcasted_iota(jnp.int32, (tokens, tokens), 1)
    ).astype(bf16)
    before = dot(one_hot.astype(bf16), earlier, 1, 0)
    rank = jnp.sum(before * one_hot, axis=0, keepdims=True).astype(jnp.int32)
    return ((distance & 1) * pairs + (pairs - (distance >> 1)) % pairs) * capacity + rank


def store_parts(rows, outs):
    start = 0
    for out in outs:
        out[...] = rows[start : start + out.shape[0]].astype(bf16)
        start += out.shape[0]


def place_kernel(capacity, pairs, routes_ref, tokens_ref, by_slot_ref, *outs):
    slots, tokens = by_slot_ref.shape
    slot = slot_row(routes_ref[...], capacity, pairs)
    by_slot = (lax.broadcasted_iota(jnp.int32, (slots, tokens), 0) == slot).astype(f32).astype(bf16)
    by_slot_ref[...] = by_slot
    store_parts(dot(by_slot, tokens_ref[...], 1, 0), outs)


def place_target_kernel(by_slot_ref, target_ref, *outs):
    by_slot = by_slot_ref[...]
    mark = (1.0 - jnp.sum(by_slot.astype(f32), axis=1, keepdims=True)) * absent_mark
    store_parts(dot(by_slot, target_ref[...], 1, 0) + mark, outs)


def place(name, kernel, first, values, sizes, with_slots):
    per_dev, features = values.shape
    slots = sum(sizes)
    steps = 2
    cols = lambda rows: pl.BlockSpec((rows, features // steps), lambda i: (0, i))
    whole = lambda *shape: pl.BlockSpec(shape, lambda i: (0, 0))
    outs = call(
        kernel,
        name,
        [jax.ShapeDtypeStruct((slots, per_dev), bf16)] * with_slots
        + [jax.ShapeDtypeStruct((size, features), bf16) for size in sizes],
        (steps,),
        [whole(*first.shape), cols(per_dev)],
        [whole(slots, per_dev)] * with_slots + [cols(size) for size in sizes],
        [],
        2 * slots * per_dev * features,
        2 * (per_dev + slots) * features,
    )(first, values)
    return outs[0], outs[with_slots:]


def clamp_parts(latent):
    squash = jax.nn.sigmoid(4.0 * latent)
    return (latent * squash).astype(bf16), squash + 4.0 * latent * squash * (1.0 - squash)


def forward_kernel(
    steps, mine, far, shift, shift_o, enc, enc_o, dec, dec_o, pre, pre_o, keep, out, act, act_o
):
    i = pl.program_id(0)
    size = mine.shape[0]

    @pl.when(i < steps)
    def _():
        x = jnp.concatenate([mine[...], far[...]], axis=0)
        part, part_o = dot(x, enc[...], 1, 0), dot(x, enc_o[...], 1, 0)

        @pl.when(i == 0)
        def _():
            pre[...] = part - shift[...]
            pre_o[...] = part_o - shift_o[...]

        @pl.when(i > 0)
        def _():
            pre[...] += part
            pre_o[...] += part_o

    @pl.when(i == steps - 1)
    def _():
        act[...] = clamp_parts(pre[...])[0]
        act_o[...] = clamp_parts(pre_o[...])[0]

    @pl.when(i >= steps)
    def _():
        part = dot(act[...], dec[...], 1, 1) + dot(act_o[...], dec_o[...], 1, 1)
        keep[...] = part[:size]
        out[...] = part[size:].astype(bf16)


def forward(mine, far, shifts, encs, decs):
    size, features = mine.shape
    latents = encs[0].shape[1]
    steps = 2
    wide = features // steps
    early = lambda i: jnp.minimum(i, steps - 1)
    late = lambda i: jnp.maximum(i - steps, 0)
    col_in = lambda rows: pl.BlockSpec((rows, wide), lambda i: (0, early(i)))
    fixed = lambda *shape: pl.BlockSpec(shape, lambda i: (0, 0))
    col_out = pl.BlockSpec((size, wide), lambda i: (0, late(i)))
    enc_in = pl.BlockSpec((wide, latents), lambda i: (early(i), 0))
    dec_in = pl.BlockSpec((wide, latents), lambda i: (late(i), 0))
    return call(
        functools.partial(forward_kernel, steps),
        "forward",
        [
            jax.ShapeDtypeStruct((2 * size, latents), f32),
            jax.ShapeDtypeStruct((2 * size, latents), f32),
            jax.ShapeDtypeStruct((size, features), f32),
            jax.ShapeDtypeStruct((size, features), bf16),
        ],
        (2 * steps,),
        [col_in(size)] * 2 + [fixed(1, latents)] * 2 + [enc_in] * 2 + [dec_in] * 2,
        [fixed(2 * size, latents), fixed(2 * size, latents), col_out, col_out],
        [pltpu.VMEM((2 * size, latents), bf16)] * 2,
        2 * 2 * 4 * size * features * latents,
        8 * features * latents + 14 * size * features,
    )(mine, far, *shifts, *encs, *decs)


def make_error(keep, across, wanted):
    recon = (keep + across.astype(f32)).astype(bf16)
    goal = wanted.astype(f32)
    error = (recon.astype(f32) - goal) * error_scale
    return recon, jnp.where(goal < 0.5 * absent_mark, error, 0.0).astype(bf16)


def gradients_kernel(tiles, count, *refs):
    errors, rows = refs[:count], refs[count : 2 * count]
    half = count // 2
    acts, slopes = refs[2 * count : 2 * count + half], refs[2 * count + half : 3 * count]
    dec, *rest = refs[3 * count :]
    summed = len(rest) > 4
    before, rest = (rest[:2], rest[2:]) if summed else ((), rest)
    act = jnp.concatenate([a[...] for a in acts], axis=0)
    slope = jnp.concatenate([s[...] for s in slopes], axis=0)
    out_enc, out_dec, out_buf, out_sems = rest
    features = errors[0].shape[1]
    wide = features // tiles
    cuts = [slice(i * wide, (i + 1) * wide) for i in range(tiles)]
    stack = lambda refs, cut: jnp.concatenate([r[:, cut] for r in refs], axis=0)

    pending = {}

    def put(n, i, left, right, out, was):
        slot = (n * tiles + i) % 3
        if slot in pending:
            pending.pop(slot).wait()
        part = dot(left, right, 0, 0)
        if summed:
            part = part + was[0, cuts[i], :].astype(f32)
        out_buf[slot] = part.astype(bf16)
        pending[slot] = pltpu.make_async_copy(
            out_buf.at[slot], out.at[0, pl.ds(i * wide, wide), :], out_sems.at[slot]
        )
        pending[slot].start()

    total = None
    for i, cut in enumerate(cuts):
        left = stack(errors, cut)
        part = dot(left, dec[cut, :], 1, 0)
        total = part if total is None else total + part
        put(0, i, left, act, out_dec, before[1] if summed else None)
    pre = (total * slope).astype(bf16)
    for i, cut in enumerate(cuts):
        put(1, i, stack(rows, cut), pre, out_enc, before[0] if summed else None)
    for copy in pending.values():
        copy.wait()


def gradients(errors, rows, acts, slopes, dec, before):
    size, features = errors[0].shape
    latents = dec.shape[1]
    tiles = 3
    count = len(errors)
    summed = len(before) > 0
    return call(
        functools.partial(gradients_kernel, tiles, count),
        "gradients_sum" if summed else "gradients",
        [jax.ShapeDtypeStruct((1, features, latents), bf16)] * 2,
        (),
        [pl.BlockSpec(memory_space=pltpu.VMEM)] * (3 * count + 1 + len(before)),
        [pl.BlockSpec(memory_space=pl.ANY)] * 2,
        [
            pltpu.VMEM((3, features // tiles, latents), bf16),
            pltpu.SemaphoreType.DMA((3,)),
        ],
        2 * 3 * count * size * features * latents,
        6 * features * latents + 4 * count * size * features,
    )(*errors, *rows, *acts, *slopes, dec, *before)


def collect_kernel(by_slot, direct, via, out):
    out[...] = dot(by_slot[...], jnp.concatenate([direct[...], via[...]], axis=0), 0, 0).astype(bf16)


def collect(by_slot, direct, via):
    slots, tokens = by_slot.shape
    features = direct.shape[1]
    steps = 2
    cols = lambda rows: pl.BlockSpec((rows, features // steps), lambda i: (0, i))
    return call(
        collect_kernel,
        "collect",
        jax.ShapeDtypeStruct((tokens, features), bf16),
        (steps,),
        [pl.BlockSpec((slots, tokens), lambda i: (0, 0)), cols(slots // 2), cols(slots // 2)],
        cols(tokens),
        [],
        2 * slots * tokens * features,
        2 * (slots + tokens) * features,
    )(by_slot, direct, via)


def local(tokens, target, routes, thresholds, enc_weight, dec_weight):
    experts = lax.axis_size("expert")
    half = lax.axis_size("dp") // 2
    per_dev, features = tokens.shape
    capacity = 3 * per_dev // (2 * experts)
    enc = enc_weight[0]
    dec = dec_weight[0]
    pairs = experts // 2
    sizes = [pairs * capacity] * 2
    by_slot, parts = place(
        "place",
        functools.partial(place_kernel, capacity, pairs),
        routes.reshape(1, per_dev),
        tokens,
        sizes,
        True,
    )
    direct, via = parts
    _, parts = place(
        "place_target",
        place_target_kernel,
        by_slot,
        target,
        sizes,
        False,
    )
    goal_direct, goal_via = parts

    def outer(v, k, step=0):
        distance = 2 * ((pairs - k) % pairs) + step
        return pass_on(v, distance) if distance else v

    def spread(parts):
        return [outer(v, k) for k, v in enumerate(parts)]

    def cut(v):
        return [v[capacity * k : capacity * (k + 1)] for k in range(pairs)]

    def join(arrays):
        return jnp.concatenate(arrays, axis=0)

    shift = 0.25 * thresholds.astype(f32)
    shift_o = swap(shift, 1)

    def gradient_sides(pre, got):
        size = pre.shape[0] // 2
        sides = [clamp_parts(jnp.concatenate([pre[c], got[c]], axis=0)) for c in (slice(size), slice(size, None))]
        return [v for side in sides for v in side]

    out_direct, goal_direct = spread(cut(direct)), cut(goal_direct)
    out_via = pass_on(via, 1)
    enc_o = swap(enc, 1)
    *out_direct, out_via, goal_via, shift_o, enc_o = gate(out_direct + [out_via, goal_via, shift_o, enc_o])
    mine0 = join(out_direct)
    out_via = spread(cut(out_via))
    far0 = swap(mine0, half)
    dec_o = swap(after(dec, enc_o), 1)
    *out_via, mine0, far0, goal_via, dec_o = gate(out_via + [mine0, far0, goal_via, dec_o])
    shifts, encs, decs = (shift, shift_o), (enc, enc_o), (dec, dec_o)
    mine1 = join(out_via)
    far1 = swap(mine1, half)
    goal_direct = spread(gate(goal_direct, dec_o))
    goal_via = pass_on(goal_via, 1)
    pre0, pre_o0, keep0, sum0 = forward(mine0, far0, shifts, encs, decs)
    *goal_direct, mine1, far1, far0, keep0, sum0, goal_via, pre_o0 = gate(
        goal_direct + [mine1, far1, far0, keep0, sum0, goal_via, pre_o0]
    )
    across0 = swap(sum0, half)
    got0 = swap(pre_o0, 1)
    goal_via = spread(cut(after(goal_via, got0)))
    pre1, pre_o1, keep1, sum1 = forward(after(mine1, got0), far1, shifts, encs, decs)
    *goal_via, across0, sum1, got0, pre_o1, mine1 = gate(goal_via + [across0, sum1, got0, pre_o1, mine1])
    across1 = swap(sum1, half)
    recon0, error0 = make_error(keep0, across0, join(goal_direct))
    home0 = spread(cut(recon0))
    got1 = swap(pre_o1, 1)
    sides0 = gradient_sides(pre0, got0)
    *home0, across1, error0, got1, sides0[0] = gate(home0 + [across1, error0, got1, sides0[0]])
    efar0, enear0 = swap(error0, half), swap(error0, 1)
    cfar0, cmine0 = swap(far0, 1), swap(mine0, 1)
    recon1, error1 = make_error(keep1, across1, join(goal_via))
    home_via = cut(recon1)
    home1 = [outer(home_via[k], k, 1) for k in range(1, pairs)]
    sides1 = gradient_sides(pre1, got1)
    *home1, home_via, error0, efar0, cfar0, cmine0, error1, sides1[0], mine1, far1 = gate(
        home1 + [home_via[0], error0, efar0, cfar0, cmine0, error1, sides1[0], mine1, far1]
    )
    efar1 = swap(error1, half)
    ecross0, enear1, cmine1 = swap(efar0, 1), swap(error1, 1), swap(mine1, 1)
    home_via, far1 = gate([home_via, far1], ecross0, enear1)
    home1 = [pass_on(home_via, 1)] + home1
    cfar1 = swap(far1, 1)
    before = gradients(
        [error0, enear0, efar0, ecross0, error1, enear1],
        [mine0, cmine0, far0, cfar0, mine1, cmine1],
        [sides0[0], sides0[2], sides1[0]],
        [sides0[1], sides0[3], sides1[1]],
        dec,
        (),
    )
    efar1, cfar1, *before = gate([efar1, cfar1, *before])
    ecross1 = swap(efar1, 1)
    homes = gate([join(home0), join(home1)], efar1)
    recon = collect(by_slot, *homes)
    grad_enc, grad_dec = gradients(
        [efar1, ecross1], [far1, cfar1], [sides1[2]], [sides1[3]], dec, before
    )
    return recon, grad_enc, grad_dec


def solution(mesh):
    in_specs = (
        P(("dp", "expert"), None),
        P(("dp", "expert"), None),
        P(("dp", "expert"), None),
        P("expert", "dp"),
        P("expert", None, "dp"),
        P("expert", None, "dp"),
    )
    out_specs = (P(("dp", "expert"), None), P("expert", None, "dp"), P("expert", None, "dp"))
    return jax.shard_map(local, mesh=mesh, in_specs=in_specs, out_specs=out_specs, check_vma=False)
```

```python
import functools

import jax
import jax.numpy as jnp
from jax import lax
from jax.experimental import pallas as pl
from jax.experimental.pallas import tpu as pltpu
from jax.sharding import PartitionSpec as P

error_scale = 0.03125
absent_mark = 1024.0
GROUPS = 2
f32 = jnp.float32
bf16 = jnp.bfloat16
VMEM_LIMIT = 36 * 1024 * 1024
WEIGH = 10


def dot(a, b, on_a, on_b):
    return lax.dot_general(a, b, (((on_a,), (on_b,)), ((), ())), preferred_element_type=f32)


def call(kernel, name, out_shape, grid, in_specs, out_specs, scratch, flops, moved):
    return pl.pallas_call(
        kernel,
        name=name,
        out_shape=out_shape,
        grid=grid,
        in_specs=in_specs,
        out_specs=out_specs,
        scratch_shapes=scratch,
        cost_estimate=pl.CostEstimate(flops=WEIGH * flops, bytes_accessed=WEIGH * moved, transcendentals=0),
        compiler_params=pltpu.CompilerParams(
            vmem_limit_bytes=VMEM_LIMIT, dimension_semantics=("arbitrary",) * len(grid) or None
        ),
    )


def swap(v, distance):
    n = lax.axis_size("dp")
    return lax.ppermute(v, "dp", [(i, i ^ distance) for i in range(n)])


def pass_on(v, distance):
    n = lax.axis_size("expert")
    return lax.ppermute(v, "expert", [(i, i ^ distance) for i in range(n)])


def after(v, *first):
    return lax.optimization_barrier((v,) + first)[0]


def gate(values, *first):
    return list(lax.optimization_barrier(tuple(values) + first)[: len(values)])


def slot_row(route_row, capacity, pairs):
    tokens = route_row.shape[1]
    distance = route_row ^ lax.axis_index("expert")
    one_hot = (lax.broadcasted_iota(jnp.int32, (2 * pairs, tokens), 0) == distance).astype(f32)
    earlier = (
        lax.broadcasted_iota(jnp.int32, (tokens, tokens), 0)
        < lax.broadcasted_iota(jnp.int32, (tokens, tokens), 1)
    ).astype(bf16)
    before = dot(one_hot.astype(bf16), earlier, 1, 0)
    rank = jnp.sum(before * one_hot, axis=0, keepdims=True).astype(jnp.int32)
    return ((distance & 1) * pairs + (pairs - (distance >> 1)) % pairs) * capacity + rank


def store_parts(rows, outs):
    start = 0
    for out in outs:
        out[...] = rows[start : start + out.shape[0]].astype(bf16)
        start += out.shape[0]


def place_kernel(capacity, pairs, routes_ref, tokens_ref, by_slot_ref, *outs):
    slots, tokens = by_slot_ref.shape
    slot = slot_row(routes_ref[...], capacity, pairs)
    by_slot = (lax.broadcasted_iota(jnp.int32, (slots, tokens), 0) == slot).astype(f32).astype(bf16)
    by_slot_ref[...] = by_slot
    store_parts(dot(by_slot, tokens_ref[...], 1, 0), outs)


def place_target_kernel(by_slot_ref, target_ref, *outs):
    by_slot = by_slot_ref[...]
    mark = (1.0 - jnp.sum(by_slot.astype(f32), axis=1, keepdims=True)) * absent_mark
    store_parts(dot(by_slot, target_ref[...], 1, 0) + mark, outs)


def place(name, kernel, first, values, sizes, with_slots):
    per_dev, features = values.shape
    slots = sum(sizes)
    steps = 2
    cols = lambda rows: pl.BlockSpec((rows, features // steps), lambda i: (0, i))
    whole = lambda *shape: pl.BlockSpec(shape, lambda i: (0, 0))
    outs = call(
        kernel,
        name,
        [jax.ShapeDtypeStruct((slots, per_dev), bf16)] * with_slots
        + [jax.ShapeDtypeStruct((size, features), bf16) for size in sizes],
        (steps,),
        [whole(*first.shape), cols(per_dev)],
        [whole(slots, per_dev)] * with_slots + [cols(size) for size in sizes],
        [],
        2 * slots * per_dev * features,
        2 * (per_dev + slots) * features,
    )(first, values)
    return outs[0], outs[with_slots:]


def clamp_parts(latent):
    squash = jax.nn.sigmoid(4.0 * latent)
    return (latent * squash).astype(bf16), squash + 4.0 * latent * squash * (1.0 - squash)


def forward_kernel(
    steps, mine, far, shift, shift_o, enc, enc_o, dec, dec_o, pre, pre_o, keep, out, act, act_o
):
    i = pl.program_id(0)
    size = mine.shape[0]

    @pl.when(i < steps)
    def _():
        x = jnp.concatenate([mine[...], far[...]], axis=0)
        part, part_o = dot(x, enc[...], 1, 0), dot(x, enc_o[...], 1, 0)

        @pl.when(i == 0)
        def _():
            pre[...] = part - shift[...]
            pre_o[...] = part_o - shift_o[...]

        @pl.when(i > 0)
        def _():
            pre[...] += part
            pre_o[...] += part_o

    @pl.when(i == steps - 1)
    def _():
        act[...] = clamp_parts(pre[...])[0]
        act_o[...] = clamp_parts(pre_o[...])[0]

    @pl.when(i >= steps)
    def _():
        part = dot(act[...], dec[...], 1, 1) + dot(act_o[...], dec_o[...], 1, 1)
        keep[...] = part[:size]
        out[...] = part[size:].astype(bf16)


def forward(mine, far, shifts, encs, decs):
    size, features = mine.shape
    latents = encs[0].shape[1]
    steps = 2
    wide = features // steps
    early = lambda i: jnp.minimum(i, steps - 1)
    late = lambda i: jnp.maximum(i - steps, 0)
    col_in = lambda rows: pl.BlockSpec((rows, wide), lambda i: (0, early(i)))
    fixed = lambda *shape: pl.BlockSpec(shape, lambda i: (0, 0))
    col_out = pl.BlockSpec((size, wide), lambda i: (0, late(i)))
    enc_in = pl.BlockSpec((wide, latents), lambda i: (early(i), 0))
    dec_in = pl.BlockSpec((wide, latents), lambda i: (late(i), 0))
    return call(
        functools.partial(forward_kernel, steps),
        "forward",
        [
            jax.ShapeDtypeStruct((2 * size, latents), f32),
            jax.ShapeDtypeStruct((2 * size, latents), f32),
            jax.ShapeDtypeStruct((size, features), f32),
            jax.ShapeDtypeStruct((size, features), bf16),
        ],
        (2 * steps,),
        [col_in(size)] * 2 + [fixed(1, latents)] * 2 + [enc_in] * 2 + [dec_in] * 2,
        [fixed(2 * size, latents), fixed(2 * size, latents), col_out, col_out],
        [pltpu.VMEM((2 * size, latents), bf16)] * 2,
        2 * 2 * 4 * size * features * latents,
        8 * features * latents + 14 * size * features,
    )(mine, far, *shifts, *encs, *decs)


def make_error(keep, across, wanted):
    recon = (keep + across.astype(f32)).astype(bf16)
    goal = wanted.astype(f32)
    error = (recon.astype(f32) - goal) * error_scale
    return recon, jnp.where(goal < 0.5 * absent_mark, error, 0.0).astype(bf16)


def gradients_kernel(tiles, count, *refs):
    errors, rows = refs[:count], refs[count : 2 * count]
    half = count // 2
    acts, slopes = refs[2 * count : 2 * count + half], refs[2 * count + half : 3 * count]
    dec, *rest = refs[3 * count :]
    summed = len(rest) > 4
    before, rest = (rest[:2], rest[2:]) if summed else ((), rest)
    act = jnp.concatenate([a[...] for a in acts], axis=0)
    slope = jnp.concatenate([s[...] for s in slopes], axis=0)
    out_enc, out_dec, out_buf, out_sems = rest
    features = errors[0].shape[1]
    wide = features // tiles
    cuts = [slice(i * wide, (i + 1) * wide) for i in range(tiles)]
    stack = lambda refs, cut: jnp.concatenate([r[:, cut] for r in refs], axis=0)

    pending = {}

    def put(n, i, left, right, out, was):
        slot = (n * tiles + i) % 3
        if slot in pending:
            pending.pop(slot).wait()
        part = dot(left, right, 0, 0)
        if summed:
            part = part + was[0, cuts[i], :].astype(f32)
        out_buf[slot] = part.astype(bf16)
        pending[slot] = pltpu.make_async_copy(
            out_buf.at[slot], out.at[0, pl.ds(i * wide, wide), :], out_sems.at[slot]
        )
        pending[slot].start()

    total = None
    for i, cut in enumerate(cuts):
        left = stack(errors, cut)
        part = dot(left, dec[cut, :], 1, 0)
        total = part if total is None else total + part
        put(0, i, left, act, out_dec, before[1] if summed else None)
    pre = (total * slope).astype(bf16)
    for i, cut in enumerate(cuts):
        put(1, i, stack(rows, cut), pre, out_enc, before[0] if summed else None)
    for copy in pending.values():
        copy.wait()


def gradients(errors, rows, acts, slopes, dec, before):
    size, features = errors[0].shape
    latents = dec.shape[1]
    tiles = 3
    count = len(errors)
    summed = len(before) > 0
    return call(
        functools.partial(gradients_kernel, tiles, count),
        "gradients_sum" if summed else "gradients",
        [jax.ShapeDtypeStruct((1, features, latents), bf16)] * 2,
        (),
        [pl.BlockSpec(memory_space=pltpu.VMEM)] * (3 * count + 1 + len(before)),
        [pl.BlockSpec(memory_space=pl.ANY)] * 2,
        [
            pltpu.VMEM((3, features // tiles, latents), bf16),
            pltpu.SemaphoreType.DMA((3,)),
        ],
        2 * 3 * count * size * features * latents,
        6 * features * latents + 4 * count * size * features,
    )(*errors, *rows, *acts, *slopes, dec, *before)


def collect_kernel(by_slot, direct, via, out):
    out[...] = dot(by_slot[...], jnp.concatenate([direct[...], via[...]], axis=0), 0, 0).astype(bf16)


def collect(by_slot, direct, via):
    slots, tokens = by_slot.shape
    features = direct.shape[1]
    steps = 2
    cols = lambda rows: pl.BlockSpec((rows, features // steps), lambda i: (0, i))
    return call(
        collect_kernel,
        "collect",
        jax.ShapeDtypeStruct((tokens, features), bf16),
        (steps,),
        [pl.BlockSpec((slots, tokens), lambda i: (0, 0)), cols(slots // 2), cols(slots // 2)],
        cols(tokens),
        [],
        2 * slots * tokens * features,
        2 * (slots + tokens) * features,
    )(by_slot, direct, via)


def local(tokens, target, routes, thresholds, enc_weight, dec_weight):
    experts = lax.axis_size("expert")
    half = lax.axis_size("dp") // 2
    per_dev, features = tokens.shape
    capacity = 3 * per_dev // (2 * experts)
    enc = enc_weight[0]
    dec = dec_weight[0]
    pairs = experts // 2
    sizes = [pairs * capacity] * 2
    by_slot, parts = place(
        "place",
        functools.partial(place_kernel, capacity, pairs),
        routes.reshape(1, per_dev),
        tokens,
        sizes,
        True,
    )
    direct, via = parts
    _, parts = place(
        "place_target",
        place_target_kernel,
        by_slot,
        target,
        sizes,
        False,
    )
    goal_direct, goal_via = parts

    def outer(v, k, step=0):
        distance = 2 * ((pairs - k) % pairs) + step
        return pass_on(v, distance) if distance else v

    def spread(parts):
        return [outer(v, k) for k, v in enumerate(parts)]

    def cut(v):
        return [v[capacity * k : capacity * (k + 1)] for k in range(pairs)]

    def join(arrays):
        return jnp.concatenate(arrays, axis=0)

    shift = 0.25 * thresholds.astype(f32)
    shift_o = swap(shift, 1)

    def gradient_sides(pre, got):
        size = pre.shape[0] // 2
        sides = [clamp_parts(jnp.concatenate([pre[c], got[c]], axis=0)) for c in (slice(size), slice(size, None))]
        return [v for side in sides for v in side]

    out_direct, goal_direct = spread(cut(direct)), cut(goal_direct)
    out_via = pass_on(via, 1)
    enc_o = swap(enc, 1)
    *out_direct, out_via, goal_via, shift_o, enc_o = gate(out_direct + [out_via, goal_via, shift_o, enc_o])
    mine0 = join(out_direct)
    out_via = spread(cut(out_via))
    far0 = swap(mine0, half)
    dec_o = swap(after(dec, enc_o), 1)
    *out_via, mine0, far0, goal_via, dec_o = gate(out_via + [mine0, far0, goal_via, dec_o])
    shifts, encs, decs = (shift, shift_o), (enc, enc_o), (dec, dec_o)
    mine1 = join(out_via)
    far1 = swap(mine1, half)
    goal_direct = spread(gate(goal_direct, dec_o))
    goal_via = pass_on(goal_via, 1)
    pre0, pre_o0, keep0, sum0 = forward(mine0, far0, shifts, encs, decs)
    *goal_direct, mine1, far1, far0, keep0, sum0, goal_via, pre_o0 = gate(
        goal_direct + [mine1, far1, far0, keep0, sum0, goal_via, pre_o0]
    )
    across0 = swap(sum0, half)
    got0 = swap(pre_o0, 1)
    goal_via = spread(cut(after(goal_via, got0)))
    pre1, pre_o1, keep1, sum1 = forward(after(mine1, got0), far1, shifts, encs, decs)
    *goal_via, across0, sum1, got0, pre_o1, mine1 = gate(goal_via + [across0, sum1, got0, pre_o1, mine1])
    across1 = swap(sum1, half)
    recon0, error0 = make_error(keep0, across0, join(goal_direct))
    home0 = spread(cut(recon0))
    got1 = swap(pre_o1, 1)
    sides0 = gradient_sides(pre0, got0)
    *home0, across1, error0, got1, sides0[0] = gate(home0 + [across1, error0, got1, sides0[0]])
    efar0, enear0 = swap(error0, half), swap(error0, 1)
    cfar0, cmine0 = swap(far0, 1), swap(mine0, 1)
    recon1, error1 = make_error(keep1, across1, join(goal_via))
    home_via = cut(recon1)
    home1 = [outer(home_via[k], k, 1) for k in range(1, pairs)]
    sides1 = gradient_sides(pre1, got1)
    *home1, home_via, error0, efar0, cfar0, cmine0, error1, sides1[0], mine1, far1 = gate(
        home1 + [home_via[0], error0, efar0, cfar0, cmine0, error1, sides1[0], mine1, far1]
    )
    split = error1.shape[0] // 2
    efar1a, efar1b = swap(error1[:split], half), swap(error1[split:], half)
    ecross0, enear1, cmine1 = swap(efar0, 1), swap(error1, 1), swap(mine1, 1)
    home_via, far1 = gate([home_via, far1], ecross0, enear1)
    home1 = [pass_on(home_via, 1)] + home1
    cfar1 = swap(far1, 1)
    before = gradients(
        [error0, enear0, efar0, ecross0, error1, enear1],
        [mine0, cmine0, far0, cfar0, mine1, cmine1],
        [sides0[0], sides0[2], sides1[0]],
        [sides0[1], sides0[3], sides1[1]],
        dec,
        (),
    )
    homes = gate([join(home0), join(home1)], before[0])
    recon = collect(by_slot, *homes)
    ecross1a = swap(after(efar1a, before[0]), 1)
    efar1b, ecross1a, cfar1, recon, *before = gate([efar1b, ecross1a, cfar1, recon, *before])
    ecross1b = swap(efar1b, 1)
    parts = lambda v: [v[: v.shape[0] // 2], v[v.shape[0] // 2 :]]
    grad_enc, grad_dec = gradients(
        [efar1a, efar1b, ecross1a, ecross1b],
        parts(far1) + parts(cfar1),
        parts(sides1[2]),
        parts(sides1[3]),
        dec,
        before,
    )
    return recon, grad_enc, grad_dec


def solution(mesh):
    in_specs = (
        P(("dp", "expert"), None),
        P(("dp", "expert"), None),
        P(("dp", "expert"), None),
        P("expert", "dp"),
        P("expert", None, "dp"),
        P("expert", None, "dp"),
    )
    out_specs = (P(("dp", "expert"), None), P("expert", None, "dp"), P("expert", None, "dp"))
    return jax.shard_map(local, mesh=mesh, in_specs=in_specs, out_specs=out_specs, check_vma=False)
```

```python
import functools

import jax
import jax.numpy as jnp
from jax import lax
from jax.experimental import pallas as pl
from jax.experimental.pallas import tpu as pltpu
from jax.sharding import PartitionSpec as P

error_scale = 0.03125
absent_mark = 1024.0
GROUPS = 2
f32 = jnp.float32
bf16 = jnp.bfloat16
VMEM_LIMIT = 32 * 1024 * 1024
WEIGH = 10


def dot(a, b, on_a, on_b):
    return lax.dot_general(a, b, (((on_a,), (on_b,)), ((), ())), preferred_element_type=f32)


def call(kernel, name, out_shape, grid, in_specs, out_specs, scratch, flops, moved):
    return pl.pallas_call(
        kernel,
        name=name,
        out_shape=out_shape,
        grid=grid,
        in_specs=in_specs,
        out_specs=out_specs,
        scratch_shapes=scratch,
        cost_estimate=pl.CostEstimate(flops=WEIGH * flops, bytes_accessed=WEIGH * moved, transcendentals=0),
        compiler_params=pltpu.CompilerParams(
            vmem_limit_bytes=VMEM_LIMIT, dimension_semantics=("arbitrary",) * len(grid) or None
        ),
    )


def swap(v, distance):
    n = lax.axis_size("dp")
    return lax.ppermute(v, "dp", [(i, i ^ distance) for i in range(n)])


def pass_on(v, distance):
    n = lax.axis_size("expert")
    return lax.ppermute(v, "expert", [(i, i ^ distance) for i in range(n)])


def after(v, *first):
    return lax.optimization_barrier((v,) + first)[0]


def gate(values, *first):
    return list(lax.optimization_barrier(tuple(values) + first)[: len(values)])


def slot_row(route_row, capacity, pairs):
    tokens = route_row.shape[1]
    distance = route_row ^ lax.axis_index("expert")
    one_hot = (lax.broadcasted_iota(jnp.int32, (2 * pairs, tokens), 0) == distance).astype(f32)
    earlier = (
        lax.broadcasted_iota(jnp.int32, (tokens, tokens), 0)
        < lax.broadcasted_iota(jnp.int32, (tokens, tokens), 1)
    ).astype(bf16)
    before = dot(one_hot.astype(bf16), earlier, 1, 0)
    rank = jnp.sum(before * one_hot, axis=0, keepdims=True).astype(jnp.int32)
    return ((distance & 1) * pairs + (pairs - (distance >> 1)) % pairs) * capacity + rank


def store_parts(rows, outs):
    start = 0
    for out in outs:
        out[...] = rows[start : start + out.shape[0]].astype(bf16)
        start += out.shape[0]


def place_kernel(capacity, pairs, routes_ref, tokens_ref, by_slot_ref, *outs):
    slots, tokens = by_slot_ref.shape
    slot = slot_row(routes_ref[...], capacity, pairs)
    by_slot = (lax.broadcasted_iota(jnp.int32, (slots, tokens), 0) == slot).astype(f32).astype(bf16)
    by_slot_ref[...] = by_slot
    store_parts(dot(by_slot, tokens_ref[...], 1, 0), outs)


def place_target_kernel(by_slot_ref, target_ref, *outs):
    by_slot = by_slot_ref[...]
    mark = (1.0 - jnp.sum(by_slot.astype(f32), axis=1, keepdims=True)) * absent_mark
    store_parts(dot(by_slot, target_ref[...], 1, 0) + mark, outs)


def place(name, kernel, first, values, sizes, with_slots):
    per_dev, features = values.shape
    slots = sum(sizes)
    steps = 2
    cols = lambda rows: pl.BlockSpec((rows, features // steps), lambda i: (0, i))
    whole = lambda *shape: pl.BlockSpec(shape, lambda i: (0, 0))
    outs = call(
        kernel,
        name,
        [jax.ShapeDtypeStruct((slots, per_dev), bf16)] * with_slots
        + [jax.ShapeDtypeStruct((size, features), bf16) for size in sizes],
        (steps,),
        [whole(*first.shape), cols(per_dev)],
        [whole(slots, per_dev)] * with_slots + [cols(size) for size in sizes],
        [],
        2 * slots * per_dev * features,
        2 * (per_dev + slots) * features,
    )(first, values)
    return outs[0], outs[with_slots:]


def clamp_parts(latent):
    squash = jax.nn.sigmoid(4.0 * latent)
    return (latent * squash).astype(bf16), squash + 4.0 * latent * squash * (1.0 - squash)


def forward_kernel(
    steps, mine, far, shift, shift_o, enc, enc_o, dec, dec_o, pre, pre_o, keep, out, act, act_o
):
    i = pl.program_id(0)
    size = mine.shape[0]

    @pl.when(i < steps)
    def _():
        x = jnp.concatenate([mine[...], far[...]], axis=0)
        part, part_o = dot(x, enc[...], 1, 0), dot(x, enc_o[...], 1, 0)

        @pl.when(i == 0)
        def _():
            pre[...] = part - shift[...]
            pre_o[...] = part_o - shift_o[...]

        @pl.when(i > 0)
        def _():
            pre[...] += part
            pre_o[...] += part_o

    @pl.when(i == steps - 1)
    def _():
        act[...] = clamp_parts(pre[...])[0]
        act_o[...] = clamp_parts(pre_o[...])[0]

    @pl.when(i >= steps)
    def _():
        part = dot(act[...], dec[...], 1, 1) + dot(act_o[...], dec_o[...], 1, 1)
        keep[...] = part[:size]
        out[...] = part[size:].astype(bf16)


def forward(mine, far, shifts, encs, decs):
    size, features = mine.shape
    latents = encs[0].shape[1]
    steps = 2
    wide = features // steps
    early = lambda i: jnp.minimum(i, steps - 1)
    late = lambda i: jnp.maximum(i - steps, 0)
    col_in = lambda rows: pl.BlockSpec((rows, wide), lambda i: (0, early(i)))
    fixed = lambda *shape: pl.BlockSpec(shape, lambda i: (0, 0))
    col_out = pl.BlockSpec((size, wide), lambda i: (0, late(i)))
    enc_in = pl.BlockSpec((wide, latents), lambda i: (early(i), 0))
    dec_in = pl.BlockSpec((wide, latents), lambda i: (late(i), 0))
    return call(
        functools.partial(forward_kernel, steps),
        "forward",
        [
            jax.ShapeDtypeStruct((2 * size, latents), f32),
            jax.ShapeDtypeStruct((2 * size, latents), f32),
            jax.ShapeDtypeStruct((size, features), f32),
            jax.ShapeDtypeStruct((size, features), bf16),
        ],
        (2 * steps,),
        [col_in(size)] * 2 + [fixed(1, latents)] * 2 + [enc_in] * 2 + [dec_in] * 2,
        [fixed(2 * size, latents), fixed(2 * size, latents), col_out, col_out],
        [pltpu.VMEM((2 * size, latents), bf16)] * 2,
        2 * 2 * 4 * size * features * latents,
        8 * features * latents + 14 * size * features,
    )(mine, far, *shifts, *encs, *decs)


def make_error(keep, across, wanted):
    recon = (keep + across.astype(f32)).astype(bf16)
    goal = wanted.astype(f32)
    error = (recon.astype(f32) - goal) * error_scale
    return recon, jnp.where(goal < 0.5 * absent_mark, error, 0.0).astype(bf16)


def gradients_kernel(tiles, count, *refs):
    errors, rows = refs[:count], refs[count : 2 * count]
    half = count // 2
    acts, slopes = refs[2 * count : 2 * count + half], refs[2 * count + half : 3 * count]
    dec, *rest = refs[3 * count :]
    summed = len(rest) > 4
    before, rest = (rest[:2], rest[2:]) if summed else ((), rest)
    act = jnp.concatenate([a[...] for a in acts], axis=0)
    slope = jnp.concatenate([s[...] for s in slopes], axis=0)
    out_enc, out_dec, out_buf, out_sems = rest
    features = errors[0].shape[1]
    wide = features // tiles
    cuts = [slice(i * wide, (i + 1) * wide) for i in range(tiles)]
    stack = lambda refs, cut: jnp.concatenate([r[:, cut] for r in refs], axis=0)

    pending = {}

    def put(n, i, left, right, out, was):
        slot = (n * tiles + i) % 3
        if slot in pending:
            pending.pop(slot).wait()
        part = dot(left, right, 0, 0)
        if summed:
            part = part + was[0, cuts[i], :].astype(f32)
        out_buf[slot] = part.astype(bf16)
        pending[slot] = pltpu.make_async_copy(
            out_buf.at[slot], out.at[0, pl.ds(i * wide, wide), :], out_sems.at[slot]
        )
        pending[slot].start()

    total = None
    for i, cut in enumerate(cuts):
        left = stack(errors, cut)
        part = dot(left, dec[cut, :], 1, 0)
        total = part if total is None else total + part
        put(0, i, left, act, out_dec, before[1] if summed else None)
    pre = (total * slope).astype(bf16)
    for i, cut in enumerate(cuts):
        put(1, i, stack(rows, cut), pre, out_enc, before[0] if summed else None)
    for copy in pending.values():
        copy.wait()


def gradients(errors, rows, acts, slopes, dec, before):
    size, features = errors[0].shape
    latents = dec.shape[1]
    tiles = 3
    count = len(errors)
    summed = len(before) > 0
    return call(
        functools.partial(gradients_kernel, tiles, count),
        "gradients_sum" if summed else "gradients",
        [jax.ShapeDtypeStruct((1, features, latents), bf16)] * 2,
        (),
        [pl.BlockSpec(memory_space=pltpu.VMEM)] * (3 * count + 1 + len(before)),
        [pl.BlockSpec(memory_space=pl.ANY)] * 2,
        [
            pltpu.VMEM((3, features // tiles, latents), bf16),
            pltpu.SemaphoreType.DMA((3,)),
        ],
        2 * 3 * count * size * features * latents,
        6 * features * latents + 4 * count * size * features,
    )(*errors, *rows, *acts, *slopes, dec, *before)


def collect_kernel(by_slot, direct, via, out):
    out[...] = dot(by_slot[...], jnp.concatenate([direct[...], via[...]], axis=0), 0, 0).astype(bf16)


def collect(by_slot, direct, via):
    slots, tokens = by_slot.shape
    features = direct.shape[1]
    steps = 2
    cols = lambda rows: pl.BlockSpec((rows, features // steps), lambda i: (0, i))
    return call(
        collect_kernel,
        "collect",
        jax.ShapeDtypeStruct((tokens, features), bf16),
        (steps,),
        [pl.BlockSpec((slots, tokens), lambda i: (0, 0)), cols(slots // 2), cols(slots // 2)],
        cols(tokens),
        [],
        2 * slots * tokens * features,
        2 * (slots + tokens) * features,
    )(by_slot, direct, via)


def local(tokens, target, routes, thresholds, enc_weight, dec_weight):
    experts = lax.axis_size("expert")
    half = lax.axis_size("dp") // 2
    per_dev, features = tokens.shape
    capacity = 3 * per_dev // (2 * experts)
    enc = enc_weight[0]
    dec = dec_weight[0]
    pairs = experts // 2
    sizes = [pairs * capacity] * 2
    by_slot, parts = place(
        "place",
        functools.partial(place_kernel, capacity, pairs),
        routes.reshape(1, per_dev),
        tokens,
        sizes,
        True,
    )
    direct, via = parts
    _, parts = place(
        "place_target",
        place_target_kernel,
        by_slot,
        target,
        sizes,
        False,
    )
    goal_direct, goal_via = parts

    def outer(v, k, step=0):
        distance = 2 * ((pairs - k) % pairs) + step
        return pass_on(v, distance) if distance else v

    def spread(parts):
        return [outer(v, k) for k, v in enumerate(parts)]

    def cut(v):
        return [v[capacity * k : capacity * (k + 1)] for k in range(pairs)]

    def join(arrays):
        return jnp.concatenate(arrays, axis=0)

    shift = 0.25 * thresholds.astype(f32)
    shift_o = swap(shift, 1)

    def gradient_sides(pre, got):
        size = pre.shape[0] // 2
        sides = [clamp_parts(jnp.concatenate([pre[c], got[c]], axis=0)) for c in (slice(size), slice(size, None))]
        return [v for side in sides for v in side]

    out_direct, goal_direct = spread(cut(direct)), cut(goal_direct)
    out_via = pass_on(via, 1)
    enc_o = swap(enc, 1)
    *out_direct, out_via, goal_via, shift_o, enc_o = gate(out_direct + [out_via, goal_via, shift_o, enc_o])
    mine0 = join(out_direct)
    out_via = spread(cut(out_via))
    far0 = swap(mine0, half)
    dec_o = swap(after(dec, enc_o), 1)
    *out_via, mine0, far0, goal_via, dec_o = gate(out_via + [mine0, far0, goal_via, dec_o])
    shifts, encs, decs = (shift, shift_o), (enc, enc_o), (dec, dec_o)
    mine1 = join(out_via)
    far1 = swap(mine1, half)
    goal_direct = spread(gate(goal_direct, dec_o))
    goal_via = pass_on(goal_via, 1)
    pre0, pre_o0, keep0, sum0 = forward(mine0, far0, shifts, encs, decs)
    *goal_direct, mine1, far1, far0, keep0, sum0, goal_via, pre_o0 = gate(
        goal_direct + [mine1, far1, far0, keep0, sum0, goal_via, pre_o0]
    )
    across0 = swap(sum0, half)
    got0 = swap(pre_o0, 1)
    goal_via = spread(cut(after(goal_via, got0)))
    pre1, pre_o1, keep1, sum1 = forward(after(mine1, got0), far1, shifts, encs, decs)
    *goal_via, across0, sum1, got0, pre_o1, mine1 = gate(goal_via + [across0, sum1, got0, pre_o1, mine1])
    across1 = swap(sum1, half)
    recon0, error0 = make_error(keep0, across0, join(goal_direct))
    home0 = spread(cut(recon0))
    got1 = swap(pre_o1, 1)
    sides0 = gradient_sides(pre0, got0)
    *home0, across1, error0, got1, sides0[0] = gate(home0 + [across1, error0, got1, sides0[0]])
    efar0, enear0 = swap(error0, half), swap(error0, 1)
    cfar0, cmine0 = swap(far0, 1), swap(mine0, 1)
    recon1, error1 = make_error(keep1, across1, join(goal_via))
    home_via = cut(recon1)
    home1 = [outer(home_via[k], k, 1) for k in range(1, pairs)]
    sides1 = gradient_sides(pre1, got1)
    *home1, home_via, error0, efar0, cfar0, cmine0, error1, sides1[0], mine1, far1 = gate(
        home1 + [home_via[0], error0, efar0, cfar0, cmine0, error1, sides1[0], mine1, far1]
    )
    split = error1.shape[0] // 2
    efar1a, efar1b = swap(error1[:split], half), swap(error1[split:], half)
    ecross0, enear1, cmine1 = swap(efar0, 1), swap(error1, 1), swap(mine1, 1)
    home_via, far1 = gate([home_via, far1], ecross0, enear1)
    home1 = [pass_on(home_via, 1)] + home1
    cfar1 = swap(far1, 1)
    before = gradients(
        [error0, enear0, efar0, ecross0, error1, enear1],
        [mine0, cmine0, far0, cfar0, mine1, cmine1],
        [sides0[0], sides0[2], sides1[0]],
        [sides0[1], sides0[3], sides1[1]],
        dec,
        (),
    )
    homes = gate([join(home0), join(home1)], before[0])
    recon = collect(by_slot, *homes)
    ecross1a = swap(after(efar1a, before[0]), 1)
    efar1b, ecross1a, cfar1, recon, *before = gate([efar1b, ecross1a, cfar1, recon, *before])
    ecross1b = swap(efar1b, 1)
    parts = lambda v: [v[: v.shape[0] // 2], v[v.shape[0] // 2 :]]
    grad_enc, grad_dec = gradients(
        [efar1a, efar1b, ecross1a, ecross1b],
        parts(far1) + parts(cfar1),
        parts(sides1[2]),
        parts(sides1[3]),
        dec,
        before,
    )
    return recon, grad_enc, grad_dec


def solution(mesh):
    in_specs = (
        P(("dp", "expert"), None),
        P(("dp", "expert"), None),
        P(("dp", "expert"), None),
        P("expert", "dp"),
        P("expert", None, "dp"),
        P("expert", None, "dp"),
    )
    out_specs = (P(("dp", "expert"), None), P("expert", None, "dp"), P("expert", None, "dp"))
    return jax.shard_map(local, mesh=mesh, in_specs=in_specs, out_specs=out_specs, check_vma=False)
```
